128 devices in a mesh: region: 16 (over y, x), slab: 8 (over z, core).
Axes of the slice: x: 4, y: 4, z: 4, core: 2. Of those that a mesh axis runs over, the one named last changes fastest.
Arguments:
- volume: bfloat16 [65536, 1024], P(('region', 'slab')), may hold values from -40 to 40
- patches: bfloat16 [65536, 1024], P(('region', 'slab')), may hold values from -6 to 6
- requests: int32 [128, 16, 1], P(('region', 'slab')), may hold values from 0 to 3
- lists: int32 [512, 4], P(('region', 'slab')), may hold values from 0 to 15, all different within a row
- counts: int32 [512], P(('region', 'slab')), may hold values from 1 to 4, 1536 in all
- w_query: bfloat16 [1024, 1024], replicated, may hold values from -0.1875 to 0.1875
- key_weight: bfloat16 [1024, 1024], replicated, may hold values from -0.1875 to 0.1875
- value_weight: bfloat16 [1024, 1024], replicated, may hold values from -0.1875 to 0.1875
- w_out: bfloat16 [1024, 1024], replicated, may hold values from -0.1875 to 0.1875
- cotangent: bfloat16 [65536, 1024], P(('region', 'slab')), may hold values from -6 to 6
Outputs:
- mixed: bfloat16 [65536, 1024], P(('region', 'slab'))
- grad_volume: bfloat16 [65536, 1024], P(('region', 'slab'))
- grad_patches: bfloat16 [65536, 1024], P(('region', 'slab'))
- grad_out_weight: float32 [1024, 1024], replicated
The draws below stay inside these ranges and needn't reach their ends.
Inputs may be any that keep to these rules, and one draw needn't show every extreme that they name: `lists`: each row names 4 different received slots.
All inputs are finite; a program needn't handle non-finite values. No bound on the sum of `counts` on one device may be relied on, other than what follows from the above.
Results may differ from the reference program's by a relative error of at most 0.015.
The reference program's roundings to bfloat16 on the way count: a program that leaves them out, or rounds other values in their place, can miss the bound.
Values may be sent and summed in bfloat16 or wider, within the bound.
No kernel may reach another device: no remote copies, remote signals or barrier semaphores. Data moves between devices by JAX's collectives and lax.ppermute only.
A program may use at most 192 MiB of HBM per device.

```python
import math
import jax
import jax.numpy as jnp
import numpy as np
from jax import lax

D = 1024
HEADS = 16
BLOCK = 128
GQ = 128
LIST = 4
CAP = 1
GDEV = 4
BLK_DEV = 4
SLOTS = 16
GROUPS = 512
QUERIES = 65536
PATCHES = 65536
N_REGION = 16
N_SLAB = 8


def draw_volume(key, part):
    key = jax.random.fold_in(key, 11)
    first = jax.random.fold_in(key, 0)
    result = jax.random.normal(first, (QUERIES, D), jnp.float32)
    return jnp.clip(result, -40.0, 40.0).astype(jnp.bfloat16)


def touch_ends(drawn, key, smallest, largest):
    spot = [jax.random.randint(jax.random.fold_in(key, axis), (), 0, length) for axis, length in enumerate(drawn.shape)]
    main_axis = drawn.shape.index(max(drawn.shape))
    next_to = spot[:main_axis] + [(spot[main_axis] + 1) % drawn.shape[main_axis]] + spot[main_axis + 1:]
    return drawn.at[tuple(spot)].set(smallest).at[tuple(next_to)].set(largest)


def block_scale(stream_key, shape, cuts, least, high):
    factor_of, own = 1.0, jax.random.fold_in(stream_key, 6)
    for dim, blocks in cuts:
        steps = jnp.exp(jax.random.uniform(jax.random.fold_in(own, dim), (blocks,), jnp.float32, least / len(cuts), high / len(cuts)))
        factor_of = factor_of * jnp.repeat(steps, shape[dim] // blocks).reshape([-1 if axis == dim else 1 for axis in range(len(shape))])
    return factor_of


def different_ones(own_key, rows, amount, top, lift):
    ranking = jax.random.permutation(jax.random.fold_in(own_key, 1), amount)
    boost = ranking
    for power in range(3):
        boost = boost * boost // amount
    boost = boost * lift // amount
    chance = jax.random.randint(jax.random.fold_in(own_key, 2), (rows, amount), 0, 4096) + boost
    sure = jax.random.permutation(jax.random.fold_in(own_key, 3), rows)[jnp.arange(amount) % rows]
    chance = jnp.where(jnp.arange(rows)[:, None] == sure[None, :], 1 << 14, chance)
    priority = chance * amount + jnp.arange(amount)
    return lax.top_k(priority.astype(jnp.int32), top)[1].astype(jnp.int32)


def split_up(number_of, total, limit, skew):
    weights = [(1 << 20) // math.isqrt(standing ** skew) + 1 for standing in range(2, number_of + 1)]
    rest, holding = total - limit - (number_of - 1), [1] * (number_of - 1)
    while rest > 0:
        movable = [i for i in range(number_of - 1) if holding[i] < limit]
        whole, remaining = sum([weights[i] for i in movable]), rest
        for i in movable:
            extra = min(limit - holding[i], max(1, remaining * weights[i] // whole), rest)
            holding[i] = holding[i] + extra
            rest = rest - extra
    return np.array([limit] + holding)


def ragged_sizes(stream_key, amount, total, most, skew):
    if amount == 2:
        one = jax.random.randint(stream_key, (), max(1, total - most), min(most, total - 1) + 1)
        return jnp.stack([one, total - one])
    sizes = jnp.asarray(split_up(amount, total, most, skew), jnp.int32)
    twos = (amount - 1) // 2
    donor, receiver = sizes[1:1 + 2 * twos:2], sizes[2:2 + 2 * twos:2]
    margin = jnp.minimum(donor - 1, most - receiver)
    shifted = jax.random.randint(jax.random.fold_in(stream_key, 1), (twos,), 0, 1 << 20) % (margin + 1)
    sizes = sizes.at[1:1 + 2 * twos:2].set(donor - shifted).at[2:2 + 2 * twos:2].set(receiver + shifted)
    return sizes[jax.random.permutation(jax.random.fold_in(stream_key, 2), amount)]


def gaussian(key, extent, deviation, limit, pieces=(), kind=jnp.bfloat16):
    factor_of = block_scale(key, extent, pieces, -0.22, 0.18) if pieces else 1.0
    values = jax.random.normal(key, extent, jnp.float32) * deviation * factor_of
    return jnp.minimum(jnp.maximum(values, -limit), limit).astype(kind)


def setup_inputs(seed: int = 0) -> dict:
    key_list = jax.random.split(jax.random.key(seed), 11)
    volume = draw_volume(jax.random.fold_in(key_list[10], 71), 0)
    patches = gaussian(key_list[1], (PATCHES, D), 1.0, 6.0, ((0, 128),))
    requests = touch_ends(jax.random.randint(key_list[2], (N_REGION * N_SLAB, N_REGION, CAP), 0, BLK_DEV), jax.random.fold_in(key_list[2], 1), 0, BLK_DEV - 1).astype(jnp.int32)
    lists = different_ones(key_list[3], GROUPS, SLOTS, LIST, 4096)
    counts = ragged_sizes(key_list[4], GROUPS, GROUPS * 3, LIST, 2).astype(jnp.int32)
    w_query = gaussian(key_list[5], (D, D), D ** -0.5, 0.1875)
    key_weight = gaussian(key_list[6], (D, D), D ** -0.5, 0.1875)
    value_weight = gaussian(key_list[7], (D, D), D ** -0.5, 0.1875)
    w_out = gaussian(key_list[8], (D, D), D ** -0.5, 0.1875)
    cotangent = gaussian(key_list[9], (QUERIES, D), 1.0, 6.0, ((0, 128),))
    return {"volume": volume, "patches": patches, "requests": requests, "lists": lists, "counts": counts, "w_query": w_query, "key_weight": key_weight, "value_weight": value_weight, "w_out": w_out, "cotangent": cotangent}


def reference(volume, patches, requests, lists, counts, w_query, key_weight, value_weight, w_out, cotangent):
    single_float = jnp.float32
    bf16 = jnp.bfloat16
    devices = N_REGION * N_SLAB
    slot_count = N_REGION * CAP
    head_dim = D // HEADS
    scale = head_dim ** -0.5
    all_keys = jnp.dot(patches, key_weight, preferred_element_type=single_float).astype(bf16).reshape(-1, BLOCK, D)
    all_values = jnp.dot(patches, value_weight, preferred_element_type=single_float).astype(bf16).reshape(-1, BLOCK, D)
    query = jnp.dot(volume, w_query, preferred_element_type=single_float).astype(bf16)
    owner_base = jnp.arange(N_REGION, dtype=jnp.int32)[:, None] * N_SLAB
    position = jnp.arange(LIST * BLOCK, dtype=jnp.int32) // BLOCK

    def one_device(carry, inputs):
        wo_sum, key_acc, value_acc = carry
        index, q_dev, c_dev, l_dev, n_dev, r_dev = inputs
        slab_index = index % N_SLAB
        blocks = ((owner_base + slab_index) * BLK_DEV + r_dev).reshape(-1).astype(jnp.int32)
        keys = all_keys[blocks]
        values = all_values[blocks]
        query_heads = q_dev.reshape(GDEV, GQ, HEADS, head_dim).astype(single_float)
        key_heads = keys[l_dev].reshape(GDEV, LIST * BLOCK, HEADS, head_dim).astype(single_float)
        value_heads = values[l_dev].reshape(GDEV, LIST * BLOCK, HEADS, head_dim).astype(single_float)
        scores = jnp.einsum("gqhd,gkhd->ghqk", query_heads, key_heads) * scale
        live = position[None, :] < n_dev[:, None]
        scores = jnp.where(live[:, None, None, :], scores, -1e30)
        top = jnp.max(scores, axis=-1, keepdims=True)
        expd = jnp.exp(scores - top)
        probs = expd / jnp.sum(expd, axis=-1, keepdims=True)
        probs_b = probs.astype(bf16)
        attended = jnp.einsum("ghqk,gkhd->gqhd", probs_b.astype(single_float), value_heads).astype(bf16)
        flat = attended.reshape(GDEV * GQ, D)
        mixed = jnp.dot(flat, w_out, preferred_element_type=single_float).astype(bf16)
        wo_sum = wo_sum + jnp.dot(flat.T, c_dev, preferred_element_type=single_float)
        grad_att = jnp.dot(c_dev, w_out.T, preferred_element_type=single_float).astype(bf16)
        grad_att_heads = grad_att.reshape(GDEV, GQ, HEADS, head_dim).astype(single_float)
        grad_prob = jnp.einsum("gqhd,gkhd->ghqk", grad_att_heads, value_heads)
        grad_score = (probs * (grad_prob - jnp.sum(probs * grad_prob, axis=-1, keepdims=True)) * scale).astype(bf16)
        grad_query = jnp.einsum("ghqk,gkhd->gqhd", grad_score.astype(single_float), key_heads).astype(bf16)
        grad_volume = jnp.dot(grad_query.reshape(GDEV * GQ, D), w_query.T, preferred_element_type=single_float).astype(bf16)
        grad_key_list = jnp.einsum("ghqk,gqhd->gkhd", grad_score.astype(single_float), query_heads)
        grad_value_list = jnp.einsum("ghqk,gqhd->gkhd", probs_b.astype(single_float), grad_att_heads)
        flat_lists = l_dev.reshape(-1).astype(jnp.int32)
        slot_keys = jnp.zeros((slot_count, BLOCK, D), single_float).at[flat_lists].add(grad_key_list.reshape(-1, BLOCK, D)).astype(bf16)
        slot_values = jnp.zeros((slot_count, BLOCK, D), single_float).at[flat_lists].add(grad_value_list.reshape(-1, BLOCK, D)).astype(bf16)
        key_acc = key_acc.at[blocks].add(slot_keys.astype(single_float))
        value_acc = value_acc.at[blocks].add(slot_values.astype(single_float))
        return (wo_sum, key_acc, value_acc), (mixed, grad_volume)

    xs = (jnp.arange(devices, dtype=jnp.int32),
          query.reshape(devices, GDEV * GQ, D),
          cotangent.reshape(devices, GDEV * GQ, D),
          lists.reshape(devices, GDEV, LIST),
          counts.reshape(devices, GDEV),
          requests)
    init = (jnp.zeros((D, D), single_float),
            jnp.zeros((PATCHES // BLOCK, BLOCK, D), single_float),
            jnp.zeros((PATCHES // BLOCK, BLOCK, D), single_float))
    (wo_sum, key_acc, value_acc), (mixed, grad_volume) = lax.scan(one_device, init, xs)
    grad_patches = (jnp.dot(key_acc.reshape(-1, D), key_weight.astype(single_float).T, precision=lax.Precision.HIGHEST)
                    + jnp.dot(value_acc.reshape(-1, D), value_weight.astype(single_float).T, precision=lax.Precision.HIGHEST)).astype(bf16)
    return mixed.reshape(-1, D), grad_volume.reshape(-1, D), grad_patches, wo_sum
```

```python
import jax
import jax.numpy as jnp
from jax import lax
from jax.experimental import pallas as pl
from jax.experimental.pallas import tpu as pltpu
from jax.sharding import PartitionSpec as P

HEADS = 16
BLOCK = 128
QUAD = 4


def nt(a, b):
    return lax.dot_general(a, b, (((1,), (1,)), ((), ())), preferred_element_type=jnp.float32)


def nn(a, b):
    return lax.dot_general(a, b, (((1,), (0,)), ((), ())), preferred_element_type=jnp.float32)


def project_kernel(x_ref, wk_ref, wv_ref, k_ref, v_ref, kt_ref, vt_ref):
    bf16 = jnp.bfloat16
    x = x_ref[0]
    quads = k_ref.shape[1]
    wide = k_ref.shape[3]
    for w_ref, out_ref, out_t_ref in ((wk_ref, k_ref, kt_ref), (wv_ref, v_ref, vt_ref)):
        for quad in range(quads):
            y = nn(x, w_ref[:, quad * wide:(quad + 1) * wide])
            out_ref[0, quad] = y.astype(bf16)
            out_t_ref[0, quad] = y.T.astype(bf16)


def project(x, wk, wv):
    slots, rows, width = x.shape
    quads = HEADS // QUAD
    wide = width // quads
    bf16 = jnp.bfloat16
    flat = jax.ShapeDtypeStruct((slots, quads, rows, wide), bf16)
    turned = jax.ShapeDtypeStruct((slots, quads, wide, rows), bf16)
    return pl.pallas_call(
        project_kernel,
        grid=(slots,),
        in_specs=[
            pl.BlockSpec((1, rows, width), lambda i: (i, 0, 0)),
            pl.BlockSpec((width, width), lambda i: (0, 0)),
            pl.BlockSpec((width, width), lambda i: (0, 0)),
        ],
        out_specs=[
            pl.BlockSpec((1, quads, rows, wide), lambda i: (i, 0, 0, 0)),
            pl.BlockSpec((1, quads, rows, wide), lambda i: (i, 0, 0, 0)),
            pl.BlockSpec((1, quads, wide, rows), lambda i: (i, 0, 0, 0)),
            pl.BlockSpec((1, quads, wide, rows), lambda i: (i, 0, 0, 0)),
        ],
        out_shape=[flat, flat, turned, turned],
        compiler_params=pltpu.CompilerParams(vmem_limit_bytes=40 * 2**20),
        cost_estimate=pl.CostEstimate(
            flops=4 * slots * rows * width * width, bytes_accessed=slots * rows * width * 10, transcendentals=0
        ),
        name="project",
    )(x, wk, wv)


def attention_kernel(
    lists_ref, counts_ref, q_ref, ga_ref, k_ref, v_ref, kt_ref, vt_ref,
    att_ref, gq_ref, dkv_ref, acc_ref,
):
    bf16 = jnp.bfloat16
    f32 = jnp.float32
    slots, quads, rows, wide = k_ref.shape
    groups, listed = lists_ref.shape
    per_group = q_ref.shape[0] // groups
    width = quads * wide
    head_dim = wide // QUAD
    keys = listed * rows

    acc_ref[...] = jnp.zeros_like(acc_ref)
    lane = lax.broadcasted_iota(jnp.int32, (per_group, wide), 1) // head_dim
    key_block = lax.broadcasted_iota(jnp.int32, (keys, QUAD * per_group), 0) // rows

    def spread(x):
        zero = jnp.zeros_like(x)
        return jnp.concatenate([jnp.where(lane == h, x, zero) for h in range(QUAD)], axis=0)

    def gather_diag(y):
        parts = []
        for pair in range(QUAD // 2):
            top = y[2 * pair * head_dim:(2 * pair + 1) * head_dim, 2 * pair * per_group:(2 * pair + 1) * per_group]
            low = y[(2 * pair + 1) * head_dim:(2 * pair + 2) * head_dim, (2 * pair + 1) * per_group:(2 * pair + 2) * per_group]
            parts.append(jnp.concatenate([top, low], axis=0).T)
        return jnp.concatenate(parts, axis=1)

    def step(i, carry):
        g = i // quads
        c = i % quads
        slot = [lists_ref[g, j] for j in range(listed)]
        count = counts_ref[g]
        at_rows = pl.ds(pl.multiple_of(g * per_group, per_group), per_group)
        at_cols = pl.ds(pl.multiple_of(c * wide, wide), wide)
        k4 = jnp.concatenate([k_ref[s, c] for s in slot], axis=0)
        v4 = jnp.concatenate([v_ref[s, c] for s in slot], axis=0)
        kt4 = jnp.concatenate([kt_ref[s, c] for s in slot], axis=1)
        vt4 = jnp.concatenate([vt_ref[s, c] for s in slot], axis=1)
        q4 = spread(q_ref[at_rows, at_cols])
        g4 = spread(ga_ref[at_rows, at_cols])
        scores = nt(k4, q4)
        scores = jnp.where(key_block < count, scores, -1e30)
        top = jnp.max(scores, axis=0, keepdims=True)
        expd = jnp.exp(scores - top)
        total = jnp.sum(expd, axis=0, keepdims=True)
        probs = expd * (1.0 / total)
        grad_prob = nt(v4, g4)
        delta = jnp.sum(probs * grad_prob, axis=0, keepdims=True)
        grad_score = (probs * (grad_prob - delta)).astype(bf16)
        probs_b = probs.astype(bf16)
        att_ref[at_rows, at_cols] = gather_diag(nn(vt4, probs_b)).astype(bf16)
        gq_ref[at_rows, at_cols] = (gather_diag(nn(kt4, grad_score)) * head_dim ** -0.5).astype(bf16)
        grad_key = nn(grad_score, q4)
        grad_value = nn(probs_b, g4)
        for j in range(listed):
            s = slot[j]
            acc_ref[s, c] += grad_key[j * rows:(j + 1) * rows]
            acc_ref[s, quads + c] += grad_value[j * rows:(j + 1) * rows]
        return carry

    lax.fori_loop(0, groups * quads, step, 0)

    def finish(s, carry):
        for c in range(2 * quads):
            dkv_ref[s, :, c * wide:(c + 1) * wide] = acc_ref[s, c].astype(bf16)
        return carry

    lax.fori_loop(0, slots, finish, 0)


def attention(lists, counts, q, ga, k, v, kt, vt):
    slots, quads, rows, wide = k.shape
    width = quads * wide
    bf16 = jnp.bfloat16
    smem = pl.BlockSpec(memory_space=pltpu.SMEM)
    vmem = pl.BlockSpec(memory_space=pltpu.VMEM)
    scores = lists.shape[0] * HEADS * (q.shape[0] // lists.shape[0]) * lists.shape[1] * rows
    return pl.pallas_call(
        attention_kernel,
        in_specs=[smem, smem] + [vmem] * 6,
        out_specs=[vmem] * 3,
        out_shape=[
            jax.ShapeDtypeStruct(q.shape, bf16),
            jax.ShapeDtypeStruct(q.shape, bf16),
            jax.ShapeDtypeStruct((slots, rows, 2 * width), bf16),
        ],
        scratch_shapes=[pltpu.VMEM((slots, 2 * quads, rows, wide), jnp.float32)],
        compiler_params=pltpu.CompilerParams(vmem_limit_bytes=60 * 2**20),
        cost_estimate=pl.CostEstimate(
            flops=12 * scores * wide, bytes_accessed=30 * 2**20, transcendentals=scores
        ),
        name="attention",
    )(lists, counts, q, ga, k, v, kt, vt)


def per_device(
    volume, patches, requests, lists, counts, w_query, key_weight, value_weight, w_out, cotangent
):
    f32 = jnp.float32
    bf16 = jnp.bfloat16
    width = volume.shape[1]
    head_dim = width // HEADS
    owned = patches.shape[0] // BLOCK
    asked = lax.all_to_all(requests, "region", split_axis=1, concat_axis=0, tiled=True)
    asked = asked.reshape(-1)
    slots = asked.shape[0]
    outgoing = patches.reshape(owned, BLOCK, width)[asked]
    blocks = lax.all_to_all(outgoing, "region", split_axis=0, concat_axis=0, tiled=True)

    query = (jnp.dot(volume, w_query, preferred_element_type=f32).astype(bf16) * head_dim ** -0.5).astype(bf16)
    grad_att = nt(cotangent, w_out).astype(bf16)
    w_both = jnp.concatenate([key_weight, value_weight], axis=1)

    k, v, kt, vt = project(blocks, key_weight, value_weight)
    attended, grad_query, slot_grads = attention(lists, counts, query, grad_att, k, v, kt, vt)

    returning = nt(slot_grads.reshape(slots * BLOCK, 2 * width), w_both).astype(bf16)
    returned = lax.all_to_all(
        returning.reshape(slots, BLOCK, width), "region", split_axis=0, concat_axis=0, tiled=True
    )
    out_terms = lax.dot_general(attended, cotangent, (((0,), (0,)), ((), ())), preferred_element_type=f32)
    grad_out_weight = lax.psum(out_terms, ("region", "slab"))
    mixed = nn(attended, w_out).astype(bf16)
    grad_volume = nt(grad_query, w_query).astype(bf16)

    holds = (asked[None, :] == jnp.arange(owned, dtype=jnp.int32)[:, None]).astype(bf16)
    grad_patches = nn(holds, returned.reshape(slots, BLOCK * width)).astype(bf16)
    return mixed, grad_volume, grad_patches.reshape(owned * BLOCK, width), grad_out_weight


def solution(mesh):
    rows = P(("region", "slab"), None)
    in_specs = (
        rows, rows, P(("region", "slab"), None, None), rows, P(("region", "slab")),
        P(), P(), P(), P(), rows,
    )
    return jax.shard_map(
        per_device, mesh=mesh, in_specs=in_specs, out_specs=(rows, rows, rows, P()), check_vma=False
    )
```

```python
import jax
import jax.numpy as jnp
from jax import lax
from jax.experimental import pallas as pl
from jax.experimental.pallas import tpu as pltpu
from jax.sharding import PartitionSpec as P

HEADS = 16
BLOCK = 128
QUAD = 4
BATCH = 4
SIDE = 4
MIB = 2**20


def nt(a, b):
    return lax.dot_general(a, b, (((1,), (1,)), ((), ())), preferred_element_type=jnp.float32)


def nn(a, b):
    return lax.dot_general(a, b, (((1,), (0,)), ((), ())), preferred_element_type=jnp.float32)


def attention_kernel(
    lists_ref, counts_ref, q_hbm, ga_hbm, x_hbm, wk_hbm, wv_hbm,
    att_ref, gq_ref, ret_hbm,
    q_ref, ga_ref, x_ref, wk_ref, wv_ref, k_ref, v_ref, kt_ref, vt_ref, acc_ref,
    used_ref, order_ref, in_sems, out_sems,
):
    bf16 = jnp.bfloat16
    slots, quads, rows, wide = k_ref.shape
    groups, listed = lists_ref.shape
    per_group = q_ref.shape[0] // groups
    head_dim = wide // QUAD

    loads = [
        pltpu.make_async_copy(src, dst, in_sems.at[i])
        for i, (src, dst) in enumerate(
            ((x_hbm, x_ref), (wk_hbm, wk_ref), (wv_hbm, wv_ref), (q_hbm, q_ref), (ga_hbm, ga_ref))
        )
    ]
    for load in loads:
        load.start()

    for s in range(slots):
        used_ref[s] = 0
    for g in range(groups):
        for j in range(listed):
            s = lists_ref[g, j]
            used_ref[s] = used_ref[s] | (j < counts_ref[g]).astype(jnp.int32)
    n_used = jnp.int32(0)
    for s in range(slots):
        order_ref[n_used] = s
        n_used = n_used + used_ref[s]
    n = n_used
    for s in range(slots):
        order_ref[n] = s
        n = n + 1 - used_ref[s]
    batches = (n_used + BATCH - 1) // BATCH

    def clear(s, carry):
        acc_ref[s] = jnp.zeros(acc_ref.shape[1:], acc_ref.dtype)
        return carry

    lax.fori_loop(0, slots, clear, 0)

    for load in loads:
        load.wait()

    def project(b, carry):
        ids = [order_ref[b * BATCH + i] for i in range(BATCH)]
        x = jnp.concatenate([x_ref[s] for s in ids], axis=0)
        for w_ref, out_ref, out_t_ref in ((wk_ref, k_ref, kt_ref), (wv_ref, v_ref, vt_ref)):
            for quad in range(quads):
                y = nn(x, w_ref[:, quad * wide:(quad + 1) * wide]).astype(bf16)
                for i, s in enumerate(ids):
                    part = y[i * rows:(i + 1) * rows]
                    out_ref[s, quad] = part
                    out_t_ref[s, quad] = part.T
        return carry

    lax.fori_loop(0, batches, project, 0)

    lane = lax.broadcasted_iota(jnp.int32, (per_group, wide), 1) // head_dim

    def spread(x):
        zero = jnp.zeros_like(x)
        return jnp.concatenate([jnp.where(lane == h, x, zero) for h in range(QUAD)], axis=0)

    def gather_diag(y):
        parts = []
        for pair in range(QUAD // 2):
            blocks = []
            for h in (2 * pair, 2 * pair + 1):
                blocks.append(y[h * head_dim:(h + 1) * head_dim, h * per_group:(h + 1) * per_group])
            parts.append(jnp.concatenate(blocks, axis=0).T)
        return jnp.concatenate(parts, axis=1)

    def step(i, carry):
        g = i // quads
        c = i % quads
        count = counts_ref[g]
        slot = [lists_ref[g, 0]] + [
            jnp.where(j < count, lists_ref[g, j], lists_ref[g, 0]) for j in range(1, listed)
        ]
        at_rows = pl.ds(pl.multiple_of(g * per_group, per_group), per_group)
        at_cols = pl.ds(pl.multiple_of(c * wide, wide), wide)
        k4 = jnp.concatenate([k_ref[s, c] for s in slot], axis=0)
        v4 = jnp.concatenate([v_ref[s, c] for s in slot], axis=0)
        kt4 = jnp.concatenate([kt_ref[s, c] for s in slot], axis=1)
        vt4 = jnp.concatenate([vt_ref[s, c] for s in slot], axis=1)
        q4 = spread(q_ref[at_rows, at_cols])
        g4 = spread(ga_ref[at_rows, at_cols])
        scores = nt(k4, q4)
        limits = [jnp.where(j < count, 3e38, -1e30) for j in range(listed)]
        scores = jnp.concatenate(
            [jnp.minimum(scores[j * rows:(j + 1) * rows], limits[j]) for j in range(listed)], axis=0
        )
        top = jnp.max(scores, axis=0, keepdims=True)
        expd = jnp.exp(scores - top)
        total = jnp.sum(expd, axis=0, keepdims=True)
        probs = expd * (1.0 / total)
        grad_prob = nt(v4, g4)
        delta = jnp.sum(probs * grad_prob, axis=0, keepdims=True)
        grad_score = (probs * (grad_prob - delta)).astype(bf16)
        probs_b = probs.astype(bf16)
        att_ref[at_rows, at_cols] = gather_diag(nn(vt4, probs_b)).astype(bf16)
        gq_ref[at_rows, at_cols] = (gather_diag(nn(kt4, grad_score)) * head_dim ** -0.5).astype(bf16)
        grad_key = nn(grad_score, q4)
        grad_value = nn(probs_b, g4)
        for j in range(listed):
            s = slot[j]
            acc_ref[s, c] += grad_key[j * rows:(j + 1) * rows]
            acc_ref[s, quads + c] += grad_value[j * rows:(j + 1) * rows]
        return carry

    lax.fori_loop(0, groups * quads, step, 0)

    def send(i, s):
        return pltpu.make_async_copy(x_ref.at[s], ret_hbm.at[s], out_sems.at[i])

    def turn_back(b, carry):
        ids = [order_ref[b * BATCH + i] for i in range(BATCH)]
        grads = [
            jnp.concatenate(
                [
                    jnp.concatenate([acc_ref[s, at + c].astype(bf16) for c in range(quads)], axis=1)
                    for s in ids
                ],
                axis=0,
            )
            for at in (0, quads)
        ]
        for c in range(quads):
            out_rows = slice(c * wide, (c + 1) * wide)
            y = (nt(grads[0], wk_ref[out_rows]) + nt(grads[1], wv_ref[out_rows])).astype(bf16)
            for i, s in enumerate(ids):
                x_ref[s, :, out_rows] = y[i * rows:(i + 1) * rows]
        for i, s in enumerate(ids):
            send(b * BATCH + i, s).start()
        return carry

    lax.fori_loop(0, batches, turn_back, 0)

    def nothing(i, carry):
        s = order_ref[i]
        x_ref[s] = jnp.zeros(x_ref.shape[1:], x_ref.dtype)
        send(i, s).start()
        return carry

    lax.fori_loop(batches * BATCH, slots, nothing, 0)

    def arrive(i, carry):
        send(i, order_ref[i]).wait()
        return carry

    lax.fori_loop(0, slots, arrive, 0)


def attention(lists, counts, q, ga, x, wk, wv):
    bf16 = jnp.bfloat16
    slots, rows, width = x.shape
    quads = HEADS // QUAD
    wide = width // quads
    smem = pl.BlockSpec(memory_space=pltpu.SMEM)
    vmem = pl.BlockSpec(memory_space=pltpu.VMEM)
    hbm = pl.BlockSpec(memory_space=pl.ANY)
    scores = HEADS * q.shape[0] * lists.shape[1] * rows
    straight = pltpu.VMEM((slots, quads, rows, wide), bf16)
    turned = pltpu.VMEM((slots, quads, wide, rows), bf16)
    return pl.pallas_call(
        attention_kernel,
        in_specs=[smem, smem] + [hbm] * 5,
        out_specs=[vmem, vmem, hbm],
        out_shape=[
            jax.ShapeDtypeStruct(q.shape, bf16),
            jax.ShapeDtypeStruct(q.shape, bf16),
            jax.ShapeDtypeStruct(x.shape, bf16),
        ],
        scratch_shapes=[
            pltpu.VMEM(q.shape, bf16), pltpu.VMEM(q.shape, bf16), pltpu.VMEM(x.shape, bf16),
            pltpu.VMEM(wk.shape, bf16), pltpu.VMEM(wv.shape, bf16),
            straight, straight, turned, turned,
            pltpu.VMEM((slots, 2 * quads, rows, wide), jnp.float32),
            pltpu.SMEM((slots + 1,), jnp.int32),
            pltpu.SMEM((slots + 1,), jnp.int32),
            pltpu.SemaphoreType.DMA((5,)),
            pltpu.SemaphoreType.DMA((slots,)),
        ],
        compiler_params=pltpu.CompilerParams(vmem_limit_bytes=60 * MIB),
        cost_estimate=pl.CostEstimate(
            flops=12 * scores * wide + 8 * slots * rows * width * width,
            bytes_accessed=20 * MIB, transcendentals=scores,
        ),
        name="attention",
    )(lists, counts, q, ga, x, wk, wv)


def settle_kernel(asked_ref, x_ref, out_ref, acc_ref):
    acc_ref[...] = jnp.zeros_like(acc_ref)
    for p in range(x_ref.shape[0]):
        acc_ref[asked_ref[p]] += x_ref[p].astype(jnp.float32)
    out_ref[...] = acc_ref[...].astype(out_ref.dtype)


def settle(asked, x, owned):
    slots, rows, width = x.shape
    cut = 32
    return pl.pallas_call(
        settle_kernel,
        grid=(rows // cut,),
        in_specs=[
            pl.BlockSpec(memory_space=pltpu.SMEM),
            pl.BlockSpec((slots, cut, width), lambda i: (0, i, 0)),
        ],
        out_specs=pl.BlockSpec((owned, cut, width), lambda i: (0, i, 0)),
        out_shape=jax.ShapeDtypeStruct((owned, rows, width), jnp.bfloat16),
        scratch_shapes=[pltpu.VMEM((owned, cut, width), jnp.float32)],
        compiler_params=pltpu.CompilerParams(vmem_limit_bytes=16 * MIB),
        cost_estimate=pl.CostEstimate(flops=slots * rows * width, bytes_accessed=3 * slots * rows * width, transcendentals=0),
        name="settle",
    )(asked, x)


def pick(parts, index):
    start = [index.astype(jnp.uint32)] + [jnp.uint32(0)] * (parts.ndim - 1)
    return lax.dynamic_slice(parts, start, (1,) + parts.shape[1:])[0]


def sum_over_devices(terms):
    f32, bf16 = jnp.float32, jnp.bfloat16
    region, slab = (lax.axis_index(axis).astype(jnp.uint32) for axis in ("region", "slab"))
    x = region & (SIDE - 1)
    z, core = slab >> 1, slab & 1
    width = terms.shape[1]

    def along_z(a, by):
        return lax.ppermute(a, "slab", [(p * 2 + c, (p + by) % SIDE * 2 + c) for p in range(SIDE) for c in range(2)])

    def along_x(a, by):
        return lax.ppermute(a, "region", [(p * SIDE + i, p * SIDE + (i + by) % SIDE) for p in range(SIDE) for i in range(SIDE)])

    def along_y(a, by):
        return lax.ppermute(a, "region", [(i * SIDE + p, (i + by) % SIDE * SIDE + p) for p in range(SIDE) for i in range(SIDE)])

    def swap(a):
        return lax.ppermute(a, "slab", [(p * 2 + c, p * 2 + 1 - c) for p in range(SIDE) for c in range(2)])

    def scatter(a, move, place):
        parts = a.reshape(SIDE, a.shape[0] // SIDE, width)
        got = [move(pick(parts, (place + by) & (SIDE - 1)).astype(bf16), by).astype(f32) for by in range(1, SIDE)]
        return pick(parts, place) + (got[0] + got[1] + got[2])

    def gather(a, move, place):
        got = [a] + [move(a, by) for by in range(1, SIDE)]
        stacked = jnp.stack(got)
        parts = [pick(stacked, (place - i) & (SIDE - 1)) for i in range(SIDE)]
        return jnp.concatenate(parts, axis=0)

    halves = terms.reshape(2, terms.shape[0] // 2, width)
    part = pick(halves, core) + swap(pick(halves, 1 - core).astype(bf16)).astype(f32)
    part = scatter(part, along_z, z)
    part = scatter(part, along_x, x).astype(bf16)
    ring = [part.astype(f32)] + [along_y(part, by).astype(f32) for by in range(1, SIDE)]
    part = ((ring[0] + ring[2]) + (ring[1] + ring[3])).astype(bf16)
    part = gather(part, along_x, x)
    part = gather(part, along_z, z)
    other = swap(part)
    first, second = jnp.where(core == 0, part, other), jnp.where(core == 0, other, part)
    return jnp.concatenate([first, second], axis=0).astype(f32)


def per_device(
    volume, patches, requests, lists, counts, w_query, key_weight, value_weight, w_out, cotangent
):
    f32 = jnp.float32
    bf16 = jnp.bfloat16
    width = volume.shape[1]
    head_dim = width // HEADS
    owned = patches.shape[0] // BLOCK
    asked = lax.all_to_all(requests, "region", split_axis=1, concat_axis=0, tiled=True)
    asked = asked.reshape(-1)
    outgoing = patches.reshape(owned, BLOCK, width)[asked]
    blocks = lax.all_to_all(outgoing, "region", split_axis=0, concat_axis=0, tiled=True)

    query = (nn(volume, w_query).astype(bf16) * head_dim ** -0.5).astype(bf16)
    grad_att = nt(cotangent, w_out).astype(bf16)

    attended, grad_query, returning = attention(lists, counts, query, grad_att, blocks, key_weight, value_weight)

    returned = lax.all_to_all(returning, "region", split_axis=0, concat_axis=0, tiled=True)
    out_terms = lax.dot_general(attended, cotangent, (((0,), (0,)), ((), ())), preferred_element_type=f32)
    grad_out_weight = sum_over_devices(out_terms)
    mixed = nn(attended, w_out).astype(bf16)
    grad_volume = nt(grad_query, w_query).astype(bf16)
    grad_patches = settle(asked, returned, owned)
    return mixed, grad_volume, grad_patches.reshape(owned * BLOCK, width), grad_out_weight


def solution(mesh):
    rows = P(("region", "slab"), None)
    in_specs = (
        rows, rows, P(("region", "slab"), None, None), rows, P(("region", "slab")),
        P(), P(), P(), P(), rows,
    )
    return jax.shard_map(
        per_device, mesh=mesh, in_specs=in_specs, out_specs=(rows, rows, rows, P()), check_vma=False
    )
```

```python
import jax
import jax.numpy as jnp
from jax import lax
from jax.experimental import pallas as pl
from jax.experimental.pallas import tpu as pltpu
from jax.sharding import PartitionSpec as P

HEADS = 16
BLOCK = 128
QUAD = 4
BATCH = 2
SIDE = 4
PIECES = 2
MIB = 2**20


def nt(a, b):
    return lax.dot_general(a, b, (((1,), (1,)), ((), ())), preferred_element_type=jnp.float32)


def nn(a, b):
    return lax.dot_general(a, b, (((1,), (0,)), ((), ())), preferred_element_type=jnp.float32)


def attention_kernel(
    lists_ref, counts_ref, core_ref, q_hbm, ga_hbm, cot_hbm, x_hbm, wk_hbm, wv_hbm,
    att_ref, gq_ref, keep_ref, give_ref, ret0_hbm, ret1_hbm,
    q_ref, ga_ref, cot_ref, att_t_ref, x_ref, wk_ref, wv_ref, k_ref, v_ref, kt_ref, vt_ref, acc_ref,
    mask_ref, used_ref, order_ref, in_sems, out_sems,
):
    bf16 = jnp.bfloat16
    slots, quads, rows, wide = k_ref.shape
    groups, listed = lists_ref.shape
    per_group = q_ref.shape[0] // groups
    head_dim = wide // QUAD

    loads = [
        pltpu.make_async_copy(src, dst, in_sems.at[i])
        for i, (src, dst) in enumerate(
            ((x_hbm, x_ref), (wk_hbm, wk_ref), (wv_hbm, wv_ref), (q_hbm, q_ref), (ga_hbm, ga_ref), (cot_hbm, cot_ref))
        )
    ]
    for load in loads:
        load.start()

    for s in range(slots):
        used_ref[s] = 0
    for g in range(groups):
        for j in range(listed):
            s = lists_ref[g, j]
            used_ref[s] = used_ref[s] | (j < counts_ref[g]).astype(jnp.int32)
    n_used = jnp.int32(0)
    for s in range(slots):
        order_ref[n_used] = s
        n_used = n_used + used_ref[s]
    n = n_used
    for s in range(slots):
        order_ref[n] = s
        n = n + 1 - used_ref[s]
    batches = (n_used + BATCH - 1) // BATCH

    def clear(s, carry):
        acc_ref[s] = jnp.zeros(acc_ref.shape[1:], acc_ref.dtype)
        return carry

    lax.fori_loop(0, slots, clear, 0)

    for load in loads:
        load.wait()

    def project(b, carry):
        ids = [order_ref[b * BATCH + i] for i in range(BATCH)]
        x = jnp.concatenate([x_ref[s] for s in ids], axis=0)
        for w_ref, out_ref, out_t_ref in ((wk_ref, k_ref, kt_ref), (wv_ref, v_ref, vt_ref)):
            for quad in range(quads):
                y = nn(x, w_ref[:, quad * wide:(quad + 1) * wide]).astype(bf16)
                for i, s in enumerate(ids):
                    part = y[i * rows:(i + 1) * rows]
                    out_ref[s, quad] = part
                    out_t_ref[s, quad] = part.T
        return carry

    lax.fori_loop(0, batches, project, 0)

    head_of_row = lax.broadcasted_iota(jnp.int32, mask_ref.shape, 0) // per_group
    head_of_lane = lax.broadcasted_iota(jnp.int32, mask_ref.shape, 1) // head_dim
    mask_ref[...] = (head_of_row == head_of_lane).astype(jnp.float32).astype(bf16)

    def spread(x):
        return jnp.concatenate([x] * QUAD, axis=0) * mask_ref[...]

    def diagonal(y):
        blocks = [
            y[h * head_dim:(h + 1) * head_dim, h * per_group:(h + 1) * per_group] for h in range(QUAD)
        ]
        return [jnp.concatenate(blocks[h:h + 2], axis=0) for h in range(0, QUAD, 2)]

    def step(i, carry):
        g = i // quads
        c = i % quads
        count = counts_ref[g]
        slot = [lists_ref[g, 0]] + [
            jnp.where(j < count, lists_ref[g, j], lists_ref[g, 0]) for j in range(1, listed)
        ]
        at_rows = pl.ds(pl.multiple_of(g * per_group, per_group), per_group)
        at_cols = pl.ds(pl.multiple_of(c * wide, wide), wide)
        k4 = jnp.concatenate([k_ref[s, c] for s in slot], axis=0)
        v4 = jnp.concatenate([v_ref[s, c] for s in slot], axis=0)
        kt4 = jnp.concatenate([kt_ref[s, c] for s in slot], axis=1)
        vt4 = jnp.concatenate([vt_ref[s, c] for s in slot], axis=1)
        q4 = spread(q_ref[at_rows, at_cols])
        g4 = spread(ga_ref[at_rows, at_cols])
        scores = nt(k4, q4)
        limits = [jnp.where(j < count, 3e38, -1e30) for j in range(listed)]
        scores = jnp.concatenate(
            [jnp.minimum(scores[j * rows:(j + 1) * rows], limits[j]) for j in range(listed)], axis=0
        )
        top = jnp.max(scores, axis=0, keepdims=True)
        expd = jnp.exp(scores - top)
        total = jnp.sum(expd, axis=0, keepdims=True)
        probs = expd * (1.0 / total)
        grad_prob = nt(v4, g4)
        delta = jnp.sum(probs * grad_prob, axis=0, keepdims=True)
        grad_score = (probs * (grad_prob - delta)).astype(bf16)
        probs_b = probs.astype(bf16)
        att_parts = diagonal(nn(vt4, probs_b))
        att_ref[at_rows, at_cols] = jnp.concatenate([y.T for y in att_parts], axis=1).astype(bf16)
        att_t_ref[at_cols, at_rows] = jnp.concatenate(att_parts, axis=0).astype(bf16)
        gq_parts = diagonal(nn(kt4, grad_score) * head_dim ** -0.5)
        gq_ref[at_rows, at_cols] = jnp.concatenate([y.T for y in gq_parts], axis=1).astype(bf16)
        grad_key = nn(grad_score, q4)
        grad_value = nn(probs_b, g4)
        for j in range(listed):
            s = slot[j]
            acc_ref[s, c] += grad_key[j * rows:(j + 1) * rows]
            acc_ref[s, quads + c] += grad_value[j * rows:(j + 1) * rows]
        return carry

    lax.fori_loop(0, groups * quads, step, 0, unroll=2)

    def send(i, s):
        cut = rows // PIECES
        return [
            pltpu.make_async_copy(x_ref.at[s, pl.ds(n * cut, cut)], ret.at[s], out_sems.at[i, n])
            for n, ret in enumerate((ret0_hbm, ret1_hbm))
        ]

    def turn_back(b, carry):
        ids = [order_ref[b * BATCH + i] for i in range(BATCH)]
        grads = [
            jnp.concatenate(
                [
                    jnp.concatenate([acc_ref[s, at + c].astype(bf16) for c in range(quads)], axis=1)
                    for s in ids
                ],
                axis=0,
            )
            for at in (0, quads)
        ]
        for c in range(quads):
            out_rows = slice(c * wide, (c + 1) * wide)
            y = (nt(grads[0], wk_ref[out_rows]) + nt(grads[1], wv_ref[out_rows])).astype(bf16)
            for i, s in enumerate(ids):
                x_ref[s, :, out_rows] = y[i * rows:(i + 1) * rows]
        for i, s in enumerate(ids):
            for copy in send(b * BATCH + i, s):
                copy.start()
        return carry

    lax.fori_loop(0, batches, turn_back, 0)

    def nothing(i, carry):
        s = order_ref[i]
        x_ref[s] = jnp.zeros(x_ref.shape[1:], x_ref.dtype)
        for copy in send(i, s):
            copy.start()
        return carry

    lax.fori_loop(batches * BATCH, slots, nothing, 0)

    half = keep_ref.shape[0]
    core = core_ref[0]
    for out_ref, mine in ((keep_ref, core), (give_ref, 1 - core)):
        for c in range(half // wide):
            at = pl.ds(pl.multiple_of(mine * half + c * wide, wide), wide)
            out_ref[c * wide:(c + 1) * wide, :] = nn(att_t_ref[at, :], cot_ref[...]).astype(out_ref.dtype)

    def arrive(i, carry):
        for copy in send(i, order_ref[i]):
            copy.wait()
        return carry

    lax.fori_loop(0, slots, arrive, 0)


def attention(lists, counts, core, q, ga, cot, x, wk, wv):
    bf16 = jnp.bfloat16
    slots, rows, width = x.shape
    quads = HEADS // QUAD
    wide = width // quads
    smem = pl.BlockSpec(memory_space=pltpu.SMEM)
    vmem = pl.BlockSpec(memory_space=pltpu.VMEM)
    hbm = pl.BlockSpec(memory_space=pl.ANY)
    scores = HEADS * q.shape[0] * lists.shape[1] * rows
    straight = pltpu.VMEM((slots, quads, rows, wide), bf16)
    turned = pltpu.VMEM((slots, quads, wide, rows), bf16)
    return pl.pallas_call(
        attention_kernel,
        in_specs=[smem] * 3 + [hbm] * 6,
        out_specs=[vmem] * 4 + [hbm] * PIECES,
        out_shape=[
            jax.ShapeDtypeStruct(q.shape, bf16),
            jax.ShapeDtypeStruct(q.shape, bf16),
            jax.ShapeDtypeStruct((width // 2, width), jnp.float32),
            jax.ShapeDtypeStruct((width // 2, width), bf16),
        ] + [jax.ShapeDtypeStruct((slots, rows // PIECES, width), bf16)] * PIECES,
        scratch_shapes=[
            pltpu.VMEM(q.shape, bf16), pltpu.VMEM(q.shape, bf16), pltpu.VMEM(q.shape, bf16),
            pltpu.VMEM(q.shape[::-1], bf16), pltpu.VMEM(x.shape, bf16),
            pltpu.VMEM(wk.shape, bf16), pltpu.VMEM(wv.shape, bf16),
            straight, straight, turned, turned,
            pltpu.VMEM((slots, 2 * quads, rows, wide), jnp.float32),
            pltpu.VMEM((QUAD * (q.shape[0] // lists.shape[0]), wide), bf16),
            pltpu.SMEM((slots + 1,), jnp.int32),
            pltpu.SMEM((slots + 1,), jnp.int32),
            pltpu.SemaphoreType.DMA((6,)),
            pltpu.SemaphoreType.DMA((slots, PIECES)),
        ],
        compiler_params=pltpu.CompilerParams(vmem_limit_bytes=62 * MIB),
        cost_estimate=pl.CostEstimate(
            flops=12 * scores * wide + 8 * slots * rows * width * width,
            bytes_accessed=20 * MIB, transcendentals=scores,
        ),
        name="attention",
    )(lists, counts, core, q, ga, cot, x, wk, wv)


def settle_kernel(asked_ref, x_ref, *refs):
    out_ref, acc_ref = refs[-2:]
    acc_ref[...] = jnp.zeros_like(acc_ref)
    for p in range(x_ref.shape[0]):
        acc_ref[asked_ref[p]] += x_ref[p].astype(jnp.float32)
    out_ref[...] = acc_ref[...].astype(out_ref.dtype)


def settle(asked, x, owned, piece, earlier=()):
    slots, rows, width = x.shape
    cut = 32
    first = piece * (rows // cut)
    return pl.pallas_call(
        settle_kernel,
        grid=(rows // cut,),
        in_specs=[
            pl.BlockSpec(memory_space=pltpu.SMEM),
            pl.BlockSpec((slots, cut, width), lambda i: (0, i, 0)),
        ] + [pl.BlockSpec(memory_space=pl.ANY)] * len(earlier),
        out_specs=pl.BlockSpec((owned, cut, width), lambda i: (0, first + i, 0)),
        out_shape=jax.ShapeDtypeStruct((owned, rows * PIECES, width), jnp.bfloat16),
        scratch_shapes=[pltpu.VMEM((owned, cut, width), jnp.float32)],
        input_output_aliases={2: 0} if earlier else {},
        compiler_params=pltpu.CompilerParams(vmem_limit_bytes=16 * MIB),
        cost_estimate=pl.CostEstimate(flops=slots * rows * width, bytes_accessed=3 * slots * rows * width, transcendentals=0),
        name="settle",
    )(asked, x, *earlier)


def pick(parts, index):
    start = [index.astype(jnp.uint32)] + [jnp.uint32(0)] * (parts.ndim - 1)
    return lax.dynamic_slice(parts, start, (1,) + parts.shape[1:])[0]


def after(a, *others):
    return lax.optimization_barrier((a,) + others)[0]


def sum_over_devices(keep, give, first_piece, send_second, others):
    f32, bf16 = jnp.float32, jnp.bfloat16
    region, slab = (lax.axis_index(axis).astype(jnp.uint32) for axis in ("region", "slab"))
    x = region & (SIDE - 1)
    z, core = slab >> 1, slab & 1
    width = keep.shape[1]

    def along_z(a, by):
        return lax.ppermute(a, "slab", [(p * 2 + c, (p + by) % SIDE * 2 + c) for p in range(SIDE) for c in range(2)])

    def along_x(a, by):
        return lax.ppermute(a, "region", [(p * SIDE + i, p * SIDE + (i + by) % SIDE) for p in range(SIDE) for i in range(SIDE)])

    def along_y(a, by):
        return lax.ppermute(a, "region", [(i * SIDE + p, (i + by) % SIDE * SIDE + p) for p in range(SIDE) for i in range(SIDE)])

    def swap(a):
        return lax.ppermute(a, "slab", [(p * 2 + c, p * 2 + 1 - c) for p in range(SIDE) for c in range(2)])

    def scatter(a, move, place):
        parts = a.reshape(SIDE, a.shape[0] // SIDE, width)
        got = [move(pick(parts, (place + by) & (SIDE - 1)).astype(bf16), by).astype(f32) for by in range(1, SIDE)]
        return pick(parts, place) + (got[0] + got[1] + got[2])

    def gather(a, move, place):
        got = [a] + [move(a, by) for by in range(1, SIDE)]
        stacked = jnp.stack(got)
        parts = [pick(stacked, (place - i) & (SIDE - 1)) for i in range(SIDE)]
        return jnp.concatenate(parts, axis=0)

    part = keep + swap(give).astype(f32)
    part = scatter(part, along_z, z)
    part = after(scatter(part, along_x, x).astype(bf16), first_piece)
    ring = [part.astype(f32)] + [along_y(part, by).astype(f32) for by in range(1, SIDE)]
    part = ((ring[0] + ring[2]) + (ring[1] + ring[3])).astype(bf16)
    part = gather(part, along_x, x)
    second_piece = send_second(part)
    part = gather(part, along_z, z)
    part = after(part, second_piece, *others)
    other = swap(part)
    first, second = jnp.where(core == 0, part, other), jnp.where(core == 0, other, part)
    return jnp.concatenate([first, second], axis=0).astype(f32), second_piece


def per_device(
    volume, patches, requests, lists, counts, w_query, key_weight, value_weight, w_out, cotangent
):
    f32 = jnp.float32
    bf16 = jnp.bfloat16
    width = volume.shape[1]
    head_dim = width // HEADS
    owned = patches.shape[0] // BLOCK
    asked = lax.all_to_all(requests, "region", split_axis=1, concat_axis=0, tiled=True)
    asked = asked.reshape(-1)
    outgoing = patches.reshape(owned, BLOCK, width)[asked]
    blocks = lax.all_to_all(outgoing, "region", split_axis=0, concat_axis=0, tiled=True)

    query = (nn(volume, w_query).astype(bf16) * head_dim ** -0.5).astype(bf16)
    grad_att = nt(cotangent, w_out).astype(bf16)

    core = (lax.axis_index("slab") & 1).reshape(1)
    attended, grad_query, keep, give, *pieces = attention(
        lists, counts, core, query, grad_att, cotangent, blocks, key_weight, value_weight
    )
    returned = lax.all_to_all(pieces[0], "region", split_axis=0, concat_axis=0, tiled=True)

    mixed = nn(attended, w_out).astype(bf16)
    grad_volume = nt(grad_query, w_query).astype(bf16)
    patches_piece = settle(asked, returned, owned, 0)

    def send_second(summed):
        return lax.all_to_all(after(pieces[1], summed), "region", split_axis=0, concat_axis=0, tiled=True)

    grad_out_weight, later = sum_over_devices(
        keep, give, returned, send_second, (mixed, grad_volume, patches_piece)
    )
    grad_patches = settle(asked, later, owned, 1, (patches_piece,))
    return mixed, grad_volume, grad_patches.reshape(owned * BLOCK, width), grad_out_weight


def solution(mesh):
    rows = P(("region", "slab"), None)
    in_specs = (
        rows, rows, P(("region", "slab"), None, None), rows, P(("region", "slab")),
        P(), P(), P(), P(), rows,
    )
    return jax.shard_map(
        per_device, mesh=mesh, in_specs=in_specs, out_specs=(rows, rows, rows, P()), check_vma=False
    )
```

```python
import jax
import jax.numpy as jnp
from jax import lax
from jax.experimental import pallas as pl
from jax.experimental.pallas import tpu as pltpu
from jax.sharding import PartitionSpec as P

HEADS = 16
BLOCK = 128
QUAD = 4
BATCH = 2
SIDE = 4
PIECES = 2
MIB = 2**20


def nt(a, b):
    return lax.dot_general(a, b, (((1,), (1,)), ((), ())), preferred_element_type=jnp.float32)


def nn(a, b):
    return lax.dot_general(a, b, (((1,), (0,)), ((), ())), preferred_element_type=jnp.float32)


def attention_kernel(
    lists_ref, counts_ref, core_ref, q_hbm, ga_hbm, cot_hbm, x_hbm, wk_hbm, wv_hbm,
    att_hbm, gq_hbm, keep_hbm, give_hbm, ret0_hbm, ret1_hbm,
    att_ref, gq_ref, keep_ref, give_ref, q_ref, ga_ref, cot_ref, att_t_ref, x_ref, wk_ref, wv_ref, k_ref, v_ref, kt_ref, vt_ref, acc_ref,
    mask_ref, used_ref, order_ref, in_sems, out_sems, result_sems,
):
    bf16 = jnp.bfloat16
    slots, quads, rows, wide = k_ref.shape
    groups, listed = lists_ref.shape
    per_group = q_ref.shape[0] // groups
    head_dim = wide // QUAD

    loads = [
        pltpu.make_async_copy(src, dst, in_sems.at[i])
        for i, (src, dst) in enumerate(
            ((wk_hbm, wk_ref), (x_hbm, x_ref), (wv_hbm, wv_ref), (q_hbm, q_ref), (ga_hbm, ga_ref), (cot_hbm, cot_ref))
        )
    ]
    for load in loads:
        load.start()

    for s in range(slots):
        used_ref[s] = 0
    for g in range(groups):
        for j in range(listed):
            s = lists_ref[g, j]
            used_ref[s] = used_ref[s] | (j < counts_ref[g]).astype(jnp.int32)
    n_used = jnp.int32(0)
    for s in range(slots):
        order_ref[n_used] = s
        n_used = n_used + used_ref[s]
    n = n_used
    for s in range(slots):
        order_ref[n] = s
        n = n + 1 - used_ref[s]
    batches = (n_used + BATCH - 1) // BATCH

    def clear(s, carry):
        acc_ref[s] = jnp.zeros(acc_ref.shape[1:], acc_ref.dtype)
        return carry

    lax.fori_loop(0, slots, clear, 0)

    def project(w_ref, out_ref, out_t_ref):
        def batch(b, carry):
            ids = [order_ref[b * BATCH + i] for i in range(BATCH)]
            x = jnp.concatenate([x_ref[s] for s in ids], axis=0)
            for quad in range(quads):
                y = nn(x, w_ref[:, quad * wide:(quad + 1) * wide]).astype(bf16)
                for i, s in enumerate(ids):
                    part = y[i * rows:(i + 1) * rows]
                    out_ref[s, quad] = part
                    out_t_ref[s, quad] = part.T
            return carry

        lax.fori_loop(0, batches, batch, 0)

    for load in loads[:2]:
        load.wait()
    project(wk_ref, k_ref, kt_ref)
    loads[2].wait()
    project(wv_ref, v_ref, vt_ref)
    for load in loads[3:]:
        load.wait()

    head_of_row = lax.broadcasted_iota(jnp.int32, mask_ref.shape, 0) // per_group
    head_of_lane = lax.broadcasted_iota(jnp.int32, mask_ref.shape, 1) // head_dim
    mask_ref[...] = (head_of_row == head_of_lane).astype(jnp.float32).astype(bf16)

    def spread(x):
        return jnp.concatenate([x] * QUAD, axis=0) * mask_ref[...]

    def diagonal(y):
        blocks = [
            y[h * head_dim:(h + 1) * head_dim, h * per_group:(h + 1) * per_group] for h in range(QUAD)
        ]
        return [jnp.concatenate(blocks[h:h + 2], axis=0) for h in range(0, QUAD, 2)]

    def step(i, carry):
        g = i // quads
        c = i % quads
        count = counts_ref[g]
        slot = [lists_ref[g, 0]] + [
            jnp.where(j < count, lists_ref[g, j], lists_ref[g, 0]) for j in range(1, listed)
        ]
        at_rows = pl.ds(pl.multiple_of(g * per_group, per_group), per_group)
        at_cols = pl.ds(pl.multiple_of(c * wide, wide), wide)
        k4 = jnp.concatenate([k_ref[s, c] for s in slot], axis=0)
        v4 = jnp.concatenate([v_ref[s, c] for s in slot], axis=0)
        kt4 = jnp.concatenate([kt_ref[s, c] for s in slot], axis=1)
        vt4 = jnp.concatenate([vt_ref[s, c] for s in slot], axis=1)
        q4 = spread(q_ref[at_rows, at_cols])
        g4 = spread(ga_ref[at_rows, at_cols])
        scores = nt(k4, q4)
        limits = [jnp.where(j < count, 3e38, -1e30) for j in range(listed)]
        scores = jnp.concatenate(
            [jnp.minimum(scores[j * rows:(j + 1) * rows], limits[j]) for j in range(listed)], axis=0
        )
        top = jnp.max(scores, axis=0, keepdims=True)
        expd = jnp.exp(scores - top)
        inverse = 1.0 / jnp.sum(expd, axis=0, keepdims=True)
        grad_prob = nt(v4, g4)
        delta = jnp.sum(expd * grad_prob, axis=0, keepdims=True) * inverse
        probs = expd * inverse
        grad_score = (probs * (grad_prob - delta)).astype(bf16)
        probs_b = probs.astype(bf16)
        def paired(wt, p):
            blocks = []
            for h in range(0, QUAD, 2):
                y = nn(wt[h * head_dim:(h + 2) * head_dim], p[:, h * per_group:(h + 2) * per_group])
                blocks.append(
                    jnp.concatenate([y[:head_dim, :per_group], y[head_dim:, per_group:]], axis=0)
                )
            return blocks

        att_parts = paired(vt4, probs_b)
        att_ref[at_rows, at_cols] = jnp.concatenate([y.T for y in att_parts], axis=1).astype(bf16)
        att_t_ref[at_cols, at_rows] = jnp.concatenate(att_parts, axis=0).astype(bf16)
        gq_parts = paired(kt4, grad_score)
        gq_ref[at_rows, at_cols] = (jnp.concatenate([y.T for y in gq_parts], axis=1) * head_dim ** -0.5).astype(bf16)
        grad_key = nn(grad_score, q4)
        grad_value = nn(probs_b, g4)
        for j in range(listed):
            s = slot[j]
            acc_ref[s, c] += grad_key[j * rows:(j + 1) * rows]
            acc_ref[s, quads + c] += grad_value[j * rows:(j + 1) * rows]
        return carry

    lax.fori_loop(0, groups * quads, step, 0, unroll=4)

    results = [
        pltpu.make_async_copy(src, dst, result_sems.at[i])
        for i, (src, dst) in enumerate(
            ((att_ref, att_hbm), (gq_ref, gq_hbm), (keep_ref, keep_hbm), (give_ref, give_hbm))
        )
    ]
    for result in results[:2]:
        result.start()

    half = keep_ref.shape[0]
    core = core_ref[0]
    for out_ref, mine in ((keep_ref, core), (give_ref, 1 - core)):
        for c in range(half // wide):
            at = pl.ds(pl.multiple_of(mine * half + c * wide, wide), wide)
            out_ref[c * wide:(c + 1) * wide, :] = nn(att_t_ref[at, :], cot_ref[...]).astype(out_ref.dtype)
    for result in results[2:]:
        result.start()

    def send(i, s):
        cut = rows // PIECES
        return [
            pltpu.make_async_copy(x_ref.at[s, pl.ds(n * cut, cut)], ret.at[s], out_sems.at[i, n])
            for n, ret in enumerate((ret0_hbm, ret1_hbm))
        ]

    def turn_back(b, carry):
        ids = [order_ref[b * BATCH + i] for i in range(BATCH)]
        grads = [
            jnp.concatenate(
                [
                    jnp.concatenate([acc_ref[s, at + c].astype(bf16) for c in range(quads)], axis=1)
                    for s in ids
                ],
                axis=0,
            )
            for at in (0, quads)
        ]
        for c in range(quads):
            out_rows = slice(c * wide, (c + 1) * wide)
            y = (nt(grads[0], wk_ref[out_rows]) + nt(grads[1], wv_ref[out_rows])).astype(bf16)
            for i, s in enumerate(ids):
                x_ref[s, :, out_rows] = y[i * rows:(i + 1) * rows]
        for i, s in enumerate(ids):
            for copy in send(b * BATCH + i, s):
                copy.start()
        return carry

    lax.fori_loop(0, batches, turn_back, 0)

    def nothing(i, carry):
        s = order_ref[i]
        x_ref[s] = jnp.zeros(x_ref.shape[1:], x_ref.dtype)
        for copy in send(i, s):
            copy.start()
        return carry

    lax.fori_loop(batches * BATCH, slots, nothing, 0)

    def arrive(i, carry):
        for copy in send(i, order_ref[i]):
            copy.wait()
        return carry

    lax.fori_loop(0, slots, arrive, 0)
    for result in results:
        result.wait()


def attention(lists, counts, core, q, ga, cot, x, wk, wv):
    bf16 = jnp.bfloat16
    slots, rows, width = x.shape
    quads = HEADS // QUAD
    wide = width // quads
    smem = pl.BlockSpec(memory_space=pltpu.SMEM)
    hbm = pl.BlockSpec(memory_space=pl.ANY)
    scores = HEADS * q.shape[0] * lists.shape[1] * rows
    straight = pltpu.VMEM((slots, quads, rows, wide), bf16)
    turned = pltpu.VMEM((slots, quads, wide, rows), bf16)
    return pl.pallas_call(
        attention_kernel,
        in_specs=[smem] * 3 + [hbm] * 6,
        out_specs=[hbm] * (4 + PIECES),
        out_shape=[
            jax.ShapeDtypeStruct(q.shape, bf16),
            jax.ShapeDtypeStruct(q.shape, bf16),
            jax.ShapeDtypeStruct((width // 2, width), jnp.float32),
            jax.ShapeDtypeStruct((width // 2, width), bf16),
        ] + [jax.ShapeDtypeStruct((slots, rows // PIECES, width), bf16)] * PIECES,
        scratch_shapes=[
            pltpu.VMEM(q.shape, bf16), pltpu.VMEM(q.shape, bf16),
            pltpu.VMEM((width // 2, width), jnp.float32), pltpu.VMEM((width // 2, width), bf16),
            pltpu.VMEM(q.shape, bf16), pltpu.VMEM(q.shape, bf16), pltpu.VMEM(q.shape, bf16),
            pltpu.VMEM(q.shape[::-1], bf16), pltpu.VMEM(x.shape, bf16),
            pltpu.VMEM(wk.shape, bf16), pltpu.VMEM(wv.shape, bf16),
            straight, straight, turned, turned,
            pltpu.VMEM((slots, 2 * quads, rows, wide), jnp.float32),
            pltpu.VMEM((QUAD * (q.shape[0] // lists.shape[0]), wide), bf16),
            pltpu.SMEM((slots + 1,), jnp.int32),
            pltpu.SMEM((slots + 1,), jnp.int32),
            pltpu.SemaphoreType.DMA((6,)),
            pltpu.SemaphoreType.DMA((slots, PIECES)),
            pltpu.SemaphoreType.DMA((4,)),
        ],
        compiler_params=pltpu.CompilerParams(vmem_limit_bytes=62 * MIB),
        cost_estimate=pl.CostEstimate(
            flops=12 * scores * wide + 8 * slots * rows * width * width,
            bytes_accessed=20 * MIB, transcendentals=scores,
        ),
        name="attention",
    )(lists, counts, core, q, ga, cot, x, wk, wv)


def settle_kernel(asked_ref, x_ref, *refs):
    out_ref, acc_ref = refs[-2:]
    acc_ref[...] = jnp.zeros_like(acc_ref)
    for p in range(x_ref.shape[0]):
        acc_ref[asked_ref[p]] += x_ref[p].astype(jnp.float32)
    out_ref[...] = acc_ref[...].astype(out_ref.dtype)


def settle(asked, x, owned, piece, earlier=()):
    slots, rows, width = x.shape
    cut = 32
    first = piece * (rows // cut)
    return pl.pallas_call(
        settle_kernel,
        grid=(rows // cut,),
        in_specs=[
            pl.BlockSpec(memory_space=pltpu.SMEM),
            pl.BlockSpec((slots, cut, width), lambda i: (0, i, 0)),
        ] + [pl.BlockSpec(memory_space=pl.ANY)] * len(earlier),
        out_specs=pl.BlockSpec((owned, cut, width), lambda i: (0, first + i, 0)),
        out_shape=jax.ShapeDtypeStruct((owned, rows * PIECES, width), jnp.bfloat16),
        scratch_shapes=[pltpu.VMEM((owned, cut, width), jnp.float32)],
        input_output_aliases={2: 0} if earlier else {},
        compiler_params=pltpu.CompilerParams(vmem_limit_bytes=16 * MIB),
        cost_estimate=pl.CostEstimate(flops=slots * rows * width, bytes_accessed=3 * slots * rows * width, transcendentals=0),
        name="settle",
    )(asked, x, *earlier)


def pick(parts, index):
    start = [index.astype(jnp.uint32)] + [jnp.uint32(0)] * (parts.ndim - 1)
    return lax.dynamic_slice(parts, start, (1,) + parts.shape[1:])[0]


def after(a, *others):
    return lax.optimization_barrier((a,) + others)[0]


def sum_over_devices(keep, give, first_piece, send_second, others):
    f32, bf16 = jnp.float32, jnp.bfloat16
    region, slab = (lax.axis_index(axis).astype(jnp.uint32) for axis in ("region", "slab"))
    x = region & (SIDE - 1)
    z, core = slab >> 1, slab & 1
    width = keep.shape[1]

    def along_z(a, by):
        return lax.ppermute(a, "slab", [(p * 2 + c, (p + by) % SIDE * 2 + c) for p in range(SIDE) for c in range(2)])

    def along_x(a, by):
        return lax.ppermute(a, "region", [(p * SIDE + i, p * SIDE + (i + by) % SIDE) for p in range(SIDE) for i in range(SIDE)])

    def along_y(a, by):
        return lax.ppermute(a, "region", [(i * SIDE + p, (i + by) % SIDE * SIDE + p) for p in range(SIDE) for i in range(SIDE)])

    def swap(a):
        return lax.ppermute(a, "slab", [(p * 2 + c, p * 2 + 1 - c) for p in range(SIDE) for c in range(2)])

    def scatter(a, move, place):
        parts = a.reshape(SIDE, a.shape[0] // SIDE, width)
        got = [move(pick(parts, (place + by) & (SIDE - 1)).astype(bf16), by).astype(f32) for by in range(1, SIDE)]
        return pick(parts, place) + (got[0] + got[1] + got[2])

    def gather(a, move, place):
        got = [a] + [move(a, by) for by in range(1, SIDE)]
        stacked = jnp.stack(got)
        parts = [pick(stacked, (place - i) & (SIDE - 1)) for i in range(SIDE)]
        return jnp.concatenate(parts, axis=0)

    part = keep + swap(give).astype(f32)
    part = scatter(part, along_z, z)
    part = after(scatter(part, along_x, x).astype(bf16), first_piece)
    ring = [part.astype(f32)] + [along_y(part, by).astype(f32) for by in range(1, SIDE)]
    part = ((ring[0] + ring[2]) + (ring[1] + ring[3])).astype(bf16)
    part = gather(part, along_x, x)
    second_piece = send_second(part)
    part = gather(part, along_z, z)
    part = after(part, second_piece, *others)
    other = swap(part)
    first, second = jnp.where(core == 0, part, other), jnp.where(core == 0, other, part)
    return jnp.concatenate([first, second], axis=0).astype(f32), second_piece


def per_device(
    volume, patches, requests, lists, counts, w_query, key_weight, value_weight, w_out, cotangent
):
    f32 = jnp.float32
    bf16 = jnp.bfloat16
    width = volume.shape[1]
    head_dim = width // HEADS
    owned = patches.shape[0] // BLOCK
    asked = lax.all_to_all(requests.reshape(-1), "region", split_axis=0, concat_axis=0, tiled=True)
    outgoing = patches.reshape(owned, BLOCK, width)[asked]
    blocks = lax.all_to_all(outgoing, "region", split_axis=0, concat_axis=0, tiled=True)

    query = (nn(volume, w_query).astype(bf16) * head_dim ** -0.5).astype(bf16)
    grad_att = nt(cotangent, w_out).astype(bf16)

    core = (lax.axis_index("slab") & 1).reshape(1)
    attended, grad_query, keep, give, *pieces = attention(
        lists, counts, core, query, grad_att, cotangent, blocks, key_weight, value_weight
    )
    returned = lax.all_to_all(pieces[0], "region", split_axis=0, concat_axis=0, tiled=True)

    mixed = nn(attended, w_out).astype(bf16)
    grad_volume = nt(grad_query, w_query).astype(bf16)
    patches_piece = settle(asked, returned, owned, 0)

    def send_second(summed):
        return lax.all_to_all(after(pieces[1], summed), "region", split_axis=0, concat_axis=0, tiled=True)

    grad_out_weight, later = sum_over_devices(
        keep, give, returned, send_second, (mixed, grad_volume, patches_piece)
    )
    grad_patches = settle(asked, later, owned, 1, (patches_piece,))
    return mixed, grad_volume, grad_patches.reshape(owned * BLOCK, width), grad_out_weight


def solution(mesh):
    rows = P(("region", "slab"), None)
    in_specs = (
        rows, rows, P(("region", "slab"), None, None), rows, P(("region", "slab")),
        P(), P(), P(), P(), rows,
    )
    return jax.shard_map(
        per_device, mesh=mesh, in_specs=in_specs, out_specs=(rows, rows, rows, P()), check_vma=False
    )
```

```python
import jax
import jax.numpy as jnp
from jax import lax
from jax.experimental import pallas as pl
from jax.experimental.pallas import tpu as pltpu
from jax.sharding import PartitionSpec as P

HEADS = 16
BLOCK = 128
QUAD = 4
BATCH = 2
SIDE = 4
PIECES = 2
MIB = 2**20


def nt(a, b):
    return lax.dot_general(a, b, (((1,), (1,)), ((), ())), preferred_element_type=jnp.float32)


def nn(a, b):
    return lax.dot_general(a, b, (((1,), (0,)), ((), ())), preferred_element_type=jnp.float32)


def attention_kernel(
    lists_ref, counts_ref, core_ref, q_hbm, ga_hbm, cot_hbm, x_hbm, wk_hbm, wv_hbm,
    att_hbm, gq_hbm, keep_hbm, give_hbm, ret0_hbm, ret1_hbm,
    att_ref, gq_ref, keep_ref, give_ref, q_ref, ga_ref, cot_ref, att_t_ref, x_ref, wk_ref, wv_ref, k_ref, v_ref, kt_ref, vt_ref, acc_ref,
    mask_ref, used_ref, order_ref, in_sems, x_sems, out_sems, result_sems,
):
    bf16 = jnp.bfloat16
    slots, quads, rows, wide = k_ref.shape
    groups, listed = lists_ref.shape
    per_group = q_ref.shape[0] // groups
    head_dim = wide // QUAD

    loads = [
        pltpu.make_async_copy(src, dst, in_sems.at[i])
        for i, (src, dst) in enumerate(
            ((wk_hbm, wk_ref), (wv_hbm, wv_ref), (q_hbm, q_ref), (ga_hbm, ga_ref), (cot_hbm, cot_ref))
        )
    ]
    loads[0].start()

    for s in range(slots):
        used_ref[s] = 0
    for g in range(groups):
        for j in range(listed):
            s = lists_ref[g, j]
            used_ref[s] = used_ref[s] | (j < counts_ref[g]).astype(jnp.int32)
    n_used = jnp.int32(0)
    for s in range(slots):
        order_ref[n_used] = s
        n_used = n_used + used_ref[s]
    n = n_used
    for s in range(slots):
        order_ref[n] = s
        n = n + 1 - used_ref[s]
    batches = (n_used + BATCH - 1) // BATCH

    def bring(i):
        s = order_ref[i]
        return pltpu.make_async_copy(x_hbm.at[s], x_ref.at[s], x_sems.at[i])

    def ask(i, carry):
        bring(i).start()
        return carry

    lax.fori_loop(0, batches * BATCH, ask, 0)
    for load in loads[1:]:
        load.start()

    def clear(s, carry):
        acc_ref[s] = jnp.zeros(acc_ref.shape[1:], acc_ref.dtype)
        return carry

    lax.fori_loop(0, slots, clear, 0)

    def project(w_ref, out_ref, out_t_ref, first):
        def batch(b, carry):
            if first:
                for i in range(BATCH):
                    bring(b * BATCH + i).wait()
            ids = [order_ref[b * BATCH + i] for i in range(BATCH)]
            x = jnp.concatenate([x_ref[s] for s in ids], axis=0)
            for quad in range(quads):
                y = nn(x, w_ref[:, quad * wide:(quad + 1) * wide]).astype(bf16)
                for i, s in enumerate(ids):
                    part = y[i * rows:(i + 1) * rows]
                    out_ref[s, quad] = part
                    out_t_ref[s, quad] = part.T
            return carry

        lax.fori_loop(0, batches, batch, 0)

    loads[0].wait()
    project(wk_ref, k_ref, kt_ref, True)
    loads[1].wait()
    project(wv_ref, v_ref, vt_ref, False)
    for load in loads[2:]:
        load.wait()

    head_of_row = lax.broadcasted_iota(jnp.int32, mask_ref.shape, 0) // per_group
    head_of_lane = lax.broadcasted_iota(jnp.int32, mask_ref.shape, 1) // head_dim
    mask_ref[...] = (head_of_row == head_of_lane).astype(jnp.float32).astype(bf16)

    def spread(x):
        return jnp.concatenate([x] * QUAD, axis=0) * mask_ref[...]

    def diagonal(y):
        blocks = [
            y[h * head_dim:(h + 1) * head_dim, h * per_group:(h + 1) * per_group] for h in range(QUAD)
        ]
        return [jnp.concatenate(blocks[h:h + 2], axis=0) for h in range(0, QUAD, 2)]

    def step(i, carry):
        g = i // quads
        c = i % quads
        count = counts_ref[g]
        slot = [lists_ref[g, 0]] + [
            jnp.where(j < count, lists_ref[g, j], lists_ref[g, 0]) for j in range(1, listed)
        ]
        at_rows = pl.ds(pl.multiple_of(g * per_group, per_group), per_group)
        at_cols = pl.ds(pl.multiple_of(c * wide, wide), wide)
        k4 = jnp.concatenate([k_ref[s, c] for s in slot], axis=0)
        v4 = jnp.concatenate([v_ref[s, c] for s in slot], axis=0)
        kt4 = jnp.concatenate([kt_ref[s, c] for s in slot], axis=1)
        vt4 = jnp.concatenate([vt_ref[s, c] for s in slot], axis=1)
        q4 = spread(q_ref[at_rows, at_cols])
        g4 = spread(ga_ref[at_rows, at_cols])
        scores = nt(k4, q4)
        limits = [jnp.where(j < count, 3e38, -1e30) for j in range(listed)]
        scores = jnp.concatenate(
            [jnp.minimum(scores[j * rows:(j + 1) * rows], limits[j]) for j in range(listed)], axis=0
        )
        top = jnp.max(scores, axis=0, keepdims=True)
        expd = jnp.exp(scores - top)
        inverse = 1.0 / jnp.sum(expd, axis=0, keepdims=True)
        grad_prob = nt(v4, g4)
        delta = jnp.sum(expd * grad_prob, axis=0, keepdims=True) * inverse
        probs = expd * inverse
        grad_score = (probs * (grad_prob - delta)).astype(bf16)
        probs_b = probs.astype(bf16)
        def paired(wt, p):
            blocks = []
            for h in range(0, QUAD, 2):
                y = nn(wt[h * head_dim:(h + 2) * head_dim], p[:, h * per_group:(h + 2) * per_group])
                blocks.append(
                    jnp.concatenate([y[:head_dim, :per_group], y[head_dim:, per_group:]], axis=0)
                )
            return blocks

        att_parts = paired(vt4, probs_b)
        att_ref[at_rows, at_cols] = jnp.concatenate([y.T for y in att_parts], axis=1).astype(bf16)
        att_t_ref[at_cols, at_rows] = jnp.concatenate(att_parts, axis=0).astype(bf16)
        gq_parts = paired(kt4, grad_score)
        gq_ref[at_rows, at_cols] = (jnp.concatenate([y.T for y in gq_parts], axis=1) * head_dim ** -0.5).astype(bf16)
        grad_key = nn(grad_score, q4)
        grad_value = nn(probs_b, g4)
        for j in range(listed):
            s = slot[j]
            acc_ref[s, c] += grad_key[j * rows:(j + 1) * rows]
            acc_ref[s, quads + c] += grad_value[j * rows:(j + 1) * rows]
        return carry

    lax.fori_loop(0, groups * quads, step, 0, unroll=4)

    results = [
        pltpu.make_async_copy(src, dst, result_sems.at[i])
        for i, (src, dst) in enumerate(
            ((att_ref, att_hbm), (gq_ref, gq_hbm), (keep_ref, keep_hbm), (give_ref, give_hbm))
        )
    ]
    for result in results[:2]:
        result.start()

    half = keep_ref.shape[0]
    core = core_ref[0]
    for out_ref, mine in ((keep_ref, core), (give_ref, 1 - core)):
        for c in range(half // wide):
            at = pl.ds(pl.multiple_of(mine * half + c * wide, wide), wide)
            out_ref[c * wide:(c + 1) * wide, :] = nn(att_t_ref[at, :], cot_ref[...]).astype(out_ref.dtype)
    for result in results[2:]:
        result.start()

    def send(i, s):
        cut = rows // PIECES
        return [
            pltpu.make_async_copy(x_ref.at[s, pl.ds(n * cut, cut)], ret.at[s], out_sems.at[i, n])
            for n, ret in enumerate((ret0_hbm, ret1_hbm))
        ]

    def turn_back(b, carry):
        ids = [order_ref[b * BATCH + i] for i in range(BATCH)]
        grads = [
            jnp.concatenate(
                [
                    jnp.concatenate([acc_ref[s, at + c].astype(bf16) for c in range(quads)], axis=1)
                    for s in ids
                ],
                axis=0,
            )
            for at in (0, quads)
        ]
        for c in range(quads):
            out_rows = slice(c * wide, (c + 1) * wide)
            y = (nt(grads[0], wk_ref[out_rows]) + nt(grads[1], wv_ref[out_rows])).astype(bf16)
            for i, s in enumerate(ids):
                x_ref[s, :, out_rows] = y[i * rows:(i + 1) * rows]
        for i, s in enumerate(ids):
            for copy in send(b * BATCH + i, s):
                copy.start()
        return carry

    lax.fori_loop(0, batches, turn_back, 0)

    def nothing(i, carry):
        s = order_ref[i]
        x_ref[s] = jnp.zeros(x_ref.shape[1:], x_ref.dtype)
        for copy in send(i, s):
            copy.start()
        return carry

    lax.fori_loop(batches * BATCH, slots, nothing, 0)

    def arrive(i, carry):
        for copy in send(i, order_ref[i]):
            copy.wait()
        return carry

    lax.fori_loop(0, slots, arrive, 0)
    for result in results:
        result.wait()


def attention(lists, counts, core, q, ga, cot, x, wk, wv):
    bf16 = jnp.bfloat16
    slots, rows, width = x.shape
    quads = HEADS // QUAD
    wide = width // quads
    smem = pl.BlockSpec(memory_space=pltpu.SMEM)
    hbm = pl.BlockSpec(memory_space=pl.ANY)
    scores = HEADS * q.shape[0] * lists.shape[1] * rows
    straight = pltpu.VMEM((slots, quads, rows, wide), bf16)
    turned = pltpu.VMEM((slots, quads, wide, rows), bf16)
    return pl.pallas_call(
        attention_kernel,
        in_specs=[smem] * 3 + [hbm] * 6,
        out_specs=[hbm] * (4 + PIECES),
        out_shape=[
            jax.ShapeDtypeStruct(q.shape, bf16),
            jax.ShapeDtypeStruct(q.shape, bf16),
            jax.ShapeDtypeStruct((width // 2, width), jnp.float32),
            jax.ShapeDtypeStruct((width // 2, width), bf16),
        ] + [jax.ShapeDtypeStruct((slots, rows // PIECES, width), bf16)] * PIECES,
        scratch_shapes=[
            pltpu.VMEM(q.shape, bf16), pltpu.VMEM(q.shape, bf16),
            pltpu.VMEM((width // 2, width), jnp.float32), pltpu.VMEM((width // 2, width), bf16),
            pltpu.VMEM(q.shape, bf16), pltpu.VMEM(q.shape, bf16), pltpu.VMEM(q.shape, bf16),
            pltpu.VMEM(q.shape[::-1], bf16), pltpu.VMEM(x.shape, bf16),
            pltpu.VMEM(wk.shape, bf16), pltpu.VMEM(wv.shape, bf16),
            straight, straight, turned, turned,
            pltpu.VMEM((slots, 2 * quads, rows, wide), jnp.float32),
            pltpu.VMEM((QUAD * (q.shape[0] // lists.shape[0]), wide), bf16),
            pltpu.SMEM((slots + 1,), jnp.int32),
            pltpu.SMEM((slots + 1,), jnp.int32),
            pltpu.SemaphoreType.DMA((5,)),
            pltpu.SemaphoreType.DMA((slots,)),
            pltpu.SemaphoreType.DMA((slots, PIECES)),
            pltpu.SemaphoreType.DMA((4,)),
        ],
        compiler_params=pltpu.CompilerParams(vmem_limit_bytes=62 * MIB),
        cost_estimate=pl.CostEstimate(
            flops=12 * scores * wide + 8 * slots * rows * width * width,
            bytes_accessed=20 * MIB, transcendentals=scores,
        ),
        name="attention",
    )(lists, counts, core, q, ga, cot, x, wk, wv)


def settle_kernel(asked_ref, x_ref, *refs):
    out_ref, acc_ref = refs[-2:]
    acc_ref[...] = jnp.zeros_like(acc_ref)
    for p in range(x_ref.shape[0]):
        acc_ref[asked_ref[p]] += x_ref[p].astype(jnp.float32)
    out_ref[...] = acc_ref[...].astype(out_ref.dtype)


def settle(asked, x, owned, piece, earlier=()):
    slots, rows, width = x.shape
    cut = 32
    first = piece * (rows // cut)
    return pl.pallas_call(
        settle_kernel,
        grid=(rows // cut,),
        in_specs=[
            pl.BlockSpec(memory_space=pltpu.SMEM),
            pl.BlockSpec((slots, cut, width), lambda i: (0, i, 0)),
        ] + [pl.BlockSpec(memory_space=pl.ANY)] * len(earlier),
        out_specs=pl.BlockSpec((owned, cut, width), lambda i: (0, first + i, 0)),
        out_shape=jax.ShapeDtypeStruct((owned, rows * PIECES, width), jnp.bfloat16),
        scratch_shapes=[pltpu.VMEM((owned, cut, width), jnp.float32)],
        input_output_aliases={2: 0} if earlier else {},
        compiler_params=pltpu.CompilerParams(vmem_limit_bytes=16 * MIB),
        cost_estimate=pl.CostEstimate(flops=slots * rows * width, bytes_accessed=3 * slots * rows * width, transcendentals=0),
        name="settle",
    )(asked, x, *earlier)


def pick(parts, index):
    start = [index.astype(jnp.uint32)] + [jnp.uint32(0)] * (parts.ndim - 1)
    return lax.dynamic_slice(parts, start, (1,) + parts.shape[1:])[0]


def after(a, *others):
    return lax.optimization_barrier((a,) + others)[0]


def lay_kernel(half_ref, x_ref, *refs):
    refs[-1][...] = x_ref[...].astype(refs[-1].dtype)


def lay(half, x, earlier=()):
    rows, width = x.shape
    cut = 128
    return pl.pallas_call(
        lay_kernel,
        grid_spec=pltpu.PrefetchScalarGridSpec(
            num_scalar_prefetch=1,
            grid=(rows // cut,),
            in_specs=[pl.BlockSpec((cut, width), lambda i, half_ref: (i, 0))]
            + [pl.BlockSpec(memory_space=pl.ANY)] * len(earlier),
            out_specs=pl.BlockSpec((cut, width), lambda i, half_ref: (half_ref[0] * (rows // cut) + i, 0)),
        ),
        out_shape=jax.ShapeDtypeStruct((2 * rows, width), jnp.float32),
        input_output_aliases={2: 0} if earlier else {},
        compiler_params=pltpu.CompilerParams(vmem_limit_bytes=16 * MIB),
        cost_estimate=pl.CostEstimate(flops=rows * width, bytes_accessed=6 * rows * width, transcendentals=0),
        name="lay",
    )(half, x, *earlier)


def sum_over_devices(keep, give, first_piece, send_second, others):
    f32, bf16 = jnp.float32, jnp.bfloat16
    region, slab = (lax.axis_index(axis).astype(jnp.uint32) for axis in ("region", "slab"))
    x = region & (SIDE - 1)
    z, core = slab >> 1, slab & 1
    width = keep.shape[1]

    def along_z(a, by):
        return lax.ppermute(a, "slab", [(p * 2 + c, (p + by) % SIDE * 2 + c) for p in range(SIDE) for c in range(2)])

    def along_x(a, by):
        return lax.ppermute(a, "region", [(p * SIDE + i, p * SIDE + (i + by) % SIDE) for p in range(SIDE) for i in range(SIDE)])

    def along_y(a, by):
        return lax.ppermute(a, "region", [(i * SIDE + p, (i + by) % SIDE * SIDE + p) for p in range(SIDE) for i in range(SIDE)])

    def swap(a):
        return lax.ppermute(a, "slab", [(p * 2 + c, p * 2 + 1 - c) for p in range(SIDE) for c in range(2)])

    def scatter(a, move, place):
        parts = a.reshape(SIDE, a.shape[0] // SIDE, width)
        got = [move(pick(parts, (place + by) & (SIDE - 1)).astype(bf16), by).astype(f32) for by in range(1, SIDE)]
        return pick(parts, place) + (got[0] + got[1] + got[2])

    def gather(a, move, place):
        got = [a] + [move(a, by) for by in range(1, SIDE)]
        stacked = jnp.stack(got)
        parts = [pick(stacked, (place - i) & (SIDE - 1)) for i in range(SIDE)]
        return jnp.concatenate(parts, axis=0)

    part = keep + swap(give).astype(f32)
    part = scatter(part, along_z, z)
    part = after(scatter(part, along_x, x).astype(bf16), first_piece)
    ring = [part.astype(f32)] + [along_y(part, by).astype(f32) for by in range(1, SIDE)]
    part = ((ring[0] + ring[2]) + (ring[1] + ring[3])).astype(bf16)
    part = gather(part, along_x, x)
    second_piece = send_second(part)
    part = gather(part, along_z, z)
    mine = core.astype(jnp.int32).reshape(1)
    laid = lay(mine, part)
    other = swap(after(part, second_piece, laid, *others))
    return lay(1 - mine, other, (laid,)), second_piece


def per_device(
    volume, patches, requests, lists, counts, w_query, key_weight, value_weight, w_out, cotangent
):
    f32 = jnp.float32
    bf16 = jnp.bfloat16
    width = volume.shape[1]
    head_dim = width // HEADS
    owned = patches.shape[0] // BLOCK
    asked = lax.all_to_all(requests.reshape(-1), "region", split_axis=0, concat_axis=0, tiled=True)
    outgoing = patches.reshape(owned, BLOCK, width)[asked]
    blocks = lax.all_to_all(outgoing, "region", split_axis=0, concat_axis=0, tiled=True)

    query = (nn(volume, w_query).astype(bf16) * head_dim ** -0.5).astype(bf16)
    grad_att = nt(cotangent, w_out).astype(bf16)

    core = (lax.axis_index("slab") & 1).reshape(1)
    attended, grad_query, keep, give, *pieces = attention(
        lists, counts, core, query, grad_att, cotangent, blocks, key_weight, value_weight
    )
    returned = lax.all_to_all(pieces[0], "region", split_axis=0, concat_axis=0, tiled=True)

    mixed = nn(attended, w_out).astype(bf16)
    grad_volume = nt(grad_query, w_query).astype(bf16)
    patches_piece = settle(asked, returned, owned, 0)

    def send_second(summed):
        return lax.all_to_all(after(pieces[1], summed), "region", split_axis=0, concat_axis=0, tiled=True)

    grad_out_weight, later = sum_over_devices(
        keep, give, returned, send_second, (mixed, grad_volume, patches_piece)
    )
    grad_patches = settle(asked, later, owned, 1, (patches_piece,))
    return mixed, grad_volume, grad_patches.reshape(owned * BLOCK, width), grad_out_weight


def solution(mesh):
    rows = P(("region", "slab"), None)
    in_specs = (
        rows, rows, P(("region", "slab"), None, None), rows, P(("region", "slab")),
        P(), P(), P(), P(), rows,
    )
    return jax.shard_map(
        per_device, mesh=mesh, in_specs=in_specs, out_specs=(rows, rows, rows, P()), check_vma=False
    )
```

```python
import jax
import jax.numpy as jnp
from jax import lax
from jax.experimental import pallas as pl
from jax.experimental.pallas import tpu as pltpu
from jax.sharding import PartitionSpec as P

HEADS = 16
BLOCK = 128
QUAD = 4
BATCH = 2
RETURN_BATCH = 4
SIDE = 4
PIECES = 2
MIB = 2**20


def nt(a, b):
    return lax.dot_general(a, b, (((1,), (1,)), ((), ())), preferred_element_type=jnp.float32)


def nn(a, b):
    return lax.dot_general(a, b, (((1,), (0,)), ((), ())), preferred_element_type=jnp.float32)


def attention_kernel(
    lists_ref, counts_ref, core_ref, q_hbm, ga_hbm, cot_hbm, x_hbm, wk_hbm, wv_hbm,
    att_hbm, gq_hbm, keep_hbm, give_hbm, ret_hbm, late_hbm,
    att_ref, gq_ref, keep_ref, give_ref, late_ref, q_ref, ga_ref, cot_ref, att_t_ref, x_ref, wk_ref, wv_ref, k_ref, v_ref, kt_ref, vt_ref, acc_ref,
    mask_ref, used_ref, order_ref, in_sems, x_sems, out_sems, result_sems,
):
    bf16 = jnp.bfloat16
    slots, quads, rows, wide = k_ref.shape
    groups, listed = lists_ref.shape
    per_group = q_ref.shape[0] // groups
    head_dim = wide // QUAD

    loads = [
        pltpu.make_async_copy(src, dst, in_sems.at[i])
        for i, (src, dst) in enumerate(
            ((wk_hbm, wk_ref), (wv_hbm, wv_ref), (q_hbm, q_ref), (ga_hbm, ga_ref), (cot_hbm, cot_ref))
        )
    ]
    loads[0].start()

    for s in range(slots):
        used_ref[s] = 0
    for g in range(groups):
        for j in range(listed):
            s = lists_ref[g, j]
            used_ref[s] = used_ref[s] | (j < counts_ref[g]).astype(jnp.int32)
    n_used = jnp.int32(0)
    for s in range(slots):
        order_ref[n_used] = s
        n_used = n_used + used_ref[s]
    n = n_used
    for s in range(slots):
        order_ref[n] = s
        n = n + 1 - used_ref[s]
    batches = (n_used + BATCH - 1) // BATCH

    def bring(i):
        s = order_ref[i]
        return pltpu.make_async_copy(x_hbm.at[s], x_ref.at[s], x_sems.at[i])

    def ask(i, carry):
        bring(i).start()
        return carry

    lax.fori_loop(0, batches * BATCH, ask, 0)
    for load in loads[1:]:
        load.start()

    def clear(s, carry):
        acc_ref[s] = jnp.zeros(acc_ref.shape[1:], acc_ref.dtype)
        return carry

    lax.fori_loop(0, slots, clear, 0)

    def project(w_ref, out_ref, out_t_ref, first):
        def batch(b, carry):
            if first:
                for i in range(BATCH):
                    bring(b * BATCH + i).wait()
            ids = [order_ref[b * BATCH + i] for i in range(BATCH)]
            x = jnp.concatenate([x_ref[s] for s in ids], axis=0)
            for quad in range(quads):
                y = nn(x, w_ref[:, quad * wide:(quad + 1) * wide]).astype(bf16)
                for i, s in enumerate(ids):
                    part = y[i * rows:(i + 1) * rows]
                    out_ref[s, quad] = part
                    out_t_ref[s, quad] = part.T
            return carry

        lax.fori_loop(0, batches, batch, 0)

    loads[0].wait()
    project(wk_ref, k_ref, kt_ref, True)
    loads[1].wait()
    project(wv_ref, v_ref, vt_ref, False)
    for load in loads[2:]:
        load.wait()

    head_of_row = lax.broadcasted_iota(jnp.int32, mask_ref.shape, 0) // per_group
    head_of_lane = lax.broadcasted_iota(jnp.int32, mask_ref.shape, 1) // head_dim
    mask_ref[...] = (head_of_row == head_of_lane).astype(jnp.float32).astype(bf16)

    def spread(x):
        return jnp.concatenate([x] * QUAD, axis=0) * mask_ref[...]

    def diagonal(y):
        blocks = [
            y[h * head_dim:(h + 1) * head_dim, h * per_group:(h + 1) * per_group] for h in range(QUAD)
        ]
        return [jnp.concatenate(blocks[h:h + 2], axis=0) for h in range(0, QUAD, 2)]

    def step(i, carry):
        g = i // quads
        c = i % quads
        count = counts_ref[g]
        slot = [lists_ref[g, 0]] + [
            jnp.where(j < count, lists_ref[g, j], lists_ref[g, 0]) for j in range(1, listed)
        ]
        at_rows = pl.ds(pl.multiple_of(g * per_group, per_group), per_group)
        at_cols = pl.ds(pl.multiple_of(c * wide, wide), wide)
        k4 = jnp.concatenate([k_ref[s, c] for s in slot], axis=0)
        v4 = jnp.concatenate([v_ref[s, c] for s in slot], axis=0)
        kt4 = jnp.concatenate([kt_ref[s, c] for s in slot], axis=1)
        vt4 = jnp.concatenate([vt_ref[s, c] for s in slot], axis=1)
        q4 = spread(q_ref[at_rows, at_cols])
        g4 = spread(ga_ref[at_rows, at_cols])
        scores = nt(k4, q4)
        limits = [jnp.where(j < count, 3e38, -1e30) for j in range(listed)]
        scores = jnp.concatenate(
            [jnp.minimum(scores[j * rows:(j + 1) * rows], limits[j]) for j in range(listed)], axis=0
        )
        top = jnp.max(scores, axis=0, keepdims=True)
        expd = jnp.exp(scores - top)
        inverse = 1.0 / jnp.sum(expd, axis=0, keepdims=True)
        grad_prob = nt(v4, g4)
        delta = jnp.sum(expd * grad_prob, axis=0, keepdims=True) * inverse
        probs = expd * inverse
        grad_score = (probs * (grad_prob - delta)).astype(bf16)
        probs_b = probs.astype(bf16)
        def paired(wt, p):
            blocks = []
            for h in range(0, QUAD, 2):
                y = nn(wt[h * head_dim:(h + 2) * head_dim], p[:, h * per_group:(h + 2) * per_group])
                blocks.append(
                    jnp.concatenate([y[:head_dim, :per_group], y[head_dim:, per_group:]], axis=0)
                )
            return blocks

        att_parts = paired(vt4, probs_b)
        att_ref[at_rows, at_cols] = jnp.concatenate([y.T for y in att_parts], axis=1).astype(bf16)
        att_t_ref[at_cols, at_rows] = jnp.concatenate(att_parts, axis=0).astype(bf16)
        gq_parts = paired(kt4, grad_score)
        gq_ref[at_rows, at_cols] = (jnp.concatenate([y.T for y in gq_parts], axis=1) * head_dim ** -0.5).astype(bf16)
        grad_key = nn(grad_score, q4)
        grad_value = nn(probs_b, g4)
        for j in range(listed):
            s = slot[j]
            acc_ref[s, c] += grad_key[j * rows:(j + 1) * rows]
            acc_ref[s, quads + c] += grad_value[j * rows:(j + 1) * rows]
        return carry

    lax.fori_loop(0, groups * quads, step, 0, unroll=4)

    results = [
        pltpu.make_async_copy(src, dst, result_sems.at[i])
        for i, (src, dst) in enumerate(
            ((att_ref, att_hbm), (gq_ref, gq_hbm), (keep_ref, keep_hbm), (give_ref, give_hbm))
        )
    ]
    for result in results[:2]:
        result.start()

    half = keep_ref.shape[0]
    core = core_ref[0]
    for out_ref, mine in ((keep_ref, core), (give_ref, 1 - core)):
        for c in range(half // wide):
            at = pl.ds(pl.multiple_of(mine * half + c * wide, wide), wide)
            out_ref[c * wide:(c + 1) * wide, :] = nn(att_t_ref[at, :], cot_ref[...]).astype(out_ref.dtype)
    for result in results[2:]:
        result.start()

    cut = rows // PIECES

    def send(i, s):
        return [
            pltpu.make_async_copy(x_ref.at[s, pl.ds(0, cut)], ret_hbm.at[s], out_sems.at[i, 0]),
            pltpu.make_async_copy(late_ref.at[s], late_hbm.at[s], out_sems.at[i, 1]),
        ]

    def turn_back(b, carry):
        ids = [order_ref[b * RETURN_BATCH + i] for i in range(RETURN_BATCH)]
        grads = [
            jnp.concatenate(
                [
                    jnp.concatenate([acc_ref[s, at + c, :cut].astype(bf16) for c in range(quads)], axis=1)
                    for s in ids
                ],
                axis=0,
            )
            for at in (0, quads)
        ]
        for c in range(quads):
            out_rows = slice(c * wide, (c + 1) * wide)
            y = (nt(grads[0], wk_ref[out_rows]) + nt(grads[1], wv_ref[out_rows])).astype(bf16)
            for i, s in enumerate(ids):
                x_ref[s, :cut, out_rows] = y[i * cut:(i + 1) * cut]
        for i, s in enumerate(ids):
            for c in range(2 * quads):
                late_ref[s, :, c * wide:(c + 1) * wide] = acc_ref[s, c, cut:].astype(bf16)
            for copy in send(b * RETURN_BATCH + i, s):
                copy.start()
        return carry

    batches = (n_used + RETURN_BATCH - 1) // RETURN_BATCH
    lax.fori_loop(0, batches, turn_back, 0)

    def nothing(i, carry):
        s = order_ref[i]
        x_ref[s, :cut] = jnp.zeros((cut,) + x_ref.shape[2:], x_ref.dtype)
        late_ref[s] = jnp.zeros(late_ref.shape[1:], late_ref.dtype)
        for copy in send(i, s):
            copy.start()
        return carry

    lax.fori_loop(batches * RETURN_BATCH, slots, nothing, 0)

    def arrive(i, carry):
        for copy in send(i, order_ref[i]):
            copy.wait()
        return carry

    lax.fori_loop(0, slots, arrive, 0)
    for result in results:
        result.wait()


def attention(lists, counts, core, q, ga, cot, x, wk, wv):
    bf16 = jnp.bfloat16
    slots, rows, width = x.shape
    quads = HEADS // QUAD
    wide = width // quads
    smem = pl.BlockSpec(memory_space=pltpu.SMEM)
    hbm = pl.BlockSpec(memory_space=pl.ANY)
    scores = HEADS * q.shape[0] * lists.shape[1] * rows
    straight = pltpu.VMEM((slots, quads, rows, wide), bf16)
    turned = pltpu.VMEM((slots, quads, wide, rows), bf16)
    return pl.pallas_call(
        attention_kernel,
        in_specs=[smem] * 3 + [hbm] * 6,
        out_specs=[hbm] * 6,
        out_shape=[
            jax.ShapeDtypeStruct(q.shape, bf16),
            jax.ShapeDtypeStruct(q.shape, bf16),
            jax.ShapeDtypeStruct((width // 2, width), jnp.float32),
            jax.ShapeDtypeStruct((width // 2, width), bf16),
            jax.ShapeDtypeStruct((slots, rows // PIECES, width), bf16),
            jax.ShapeDtypeStruct((slots, rows // PIECES, 2 * width), bf16),
        ],
        scratch_shapes=[
            pltpu.VMEM(q.shape, bf16), pltpu.VMEM(q.shape, bf16),
            pltpu.VMEM((width // 2, width), jnp.float32), pltpu.VMEM((width // 2, width), bf16),
            pltpu.VMEM((slots, rows // PIECES, 2 * width), bf16),
            pltpu.VMEM(q.shape, bf16), pltpu.VMEM(q.shape, bf16), pltpu.VMEM(q.shape, bf16),
            pltpu.VMEM(q.shape[::-1], bf16), pltpu.VMEM(x.shape, bf16),
            pltpu.VMEM(wk.shape, bf16), pltpu.VMEM(wv.shape, bf16),
            straight, straight, turned, turned,
            pltpu.VMEM((slots, 2 * quads, rows, wide), jnp.float32),
            pltpu.VMEM((QUAD * (q.shape[0] // lists.shape[0]), wide), bf16),
            pltpu.SMEM((slots + 1,), jnp.int32),
            pltpu.SMEM((slots + 1,), jnp.int32),
            pltpu.SemaphoreType.DMA((5,)),
            pltpu.SemaphoreType.DMA((slots,)),
            pltpu.SemaphoreType.DMA((slots, PIECES)),
            pltpu.SemaphoreType.DMA((4,)),
        ],
        compiler_params=pltpu.CompilerParams(vmem_limit_bytes=62 * MIB),
        cost_estimate=pl.CostEstimate(
            flops=12 * scores * wide + 8 * slots * rows * width * width,
            bytes_accessed=20 * MIB, transcendentals=scores,
        ),
        name="attention",
    )(lists, counts, core, q, ga, cot, x, wk, wv)


def settle_kernel(asked_ref, x_ref, *refs):
    out_ref, acc_ref = refs[-2:]
    acc_ref[...] = jnp.zeros_like(acc_ref)
    for p in range(x_ref.shape[0]):
        acc_ref[asked_ref[p]] += x_ref[p].astype(jnp.float32)
    out_ref[...] = acc_ref[...].astype(out_ref.dtype)


def settle(asked, x, owned, piece, earlier=()):
    slots, rows, width = x.shape
    cut = 32
    first = piece * (rows // cut)
    return pl.pallas_call(
        settle_kernel,
        grid=(rows // cut,),
        in_specs=[
            pl.BlockSpec(memory_space=pltpu.SMEM),
            pl.BlockSpec((slots, cut, width), lambda i: (0, i, 0)),
        ] + [pl.BlockSpec(memory_space=pl.ANY)] * len(earlier),
        out_specs=pl.BlockSpec((owned, cut, width), lambda i: (0, first + i, 0)),
        out_shape=jax.ShapeDtypeStruct((owned, rows * PIECES, width), jnp.bfloat16),
        scratch_shapes=[pltpu.VMEM((owned, cut, width), jnp.float32)],
        input_output_aliases={2: 0} if earlier else {},
        compiler_params=pltpu.CompilerParams(vmem_limit_bytes=16 * MIB),
        cost_estimate=pl.CostEstimate(flops=slots * rows * width, bytes_accessed=3 * slots * rows * width, transcendentals=0),
        name="settle",
    )(asked, x, *earlier)


def pick(parts, index):
    start = [index.astype(jnp.uint32)] + [jnp.uint32(0)] * (parts.ndim - 1)
    return lax.dynamic_slice(parts, start, (1,) + parts.shape[1:])[0]


def after(a, *others):
    return lax.optimization_barrier((a,) + others)[0]


def lay_kernel(half_ref, x_ref, *refs):
    refs[-1][...] = x_ref[...].astype(refs[-1].dtype)


def lay(half, x, earlier=()):
    rows, width = x.shape
    cut = 128
    return pl.pallas_call(
        lay_kernel,
        grid_spec=pltpu.PrefetchScalarGridSpec(
            num_scalar_prefetch=1,
            grid=(rows // cut,),
            in_specs=[pl.BlockSpec((cut, width), lambda i, half_ref: (i, 0))]
            + [pl.BlockSpec(memory_space=pl.ANY)] * len(earlier),
            out_specs=pl.BlockSpec((cut, width), lambda i, half_ref: (half_ref[0] * (rows // cut) + i, 0)),
        ),
        out_shape=jax.ShapeDtypeStruct((2 * rows, width), jnp.float32),
        input_output_aliases={2: 0} if earlier else {},
        compiler_params=pltpu.CompilerParams(vmem_limit_bytes=16 * MIB),
        cost_estimate=pl.CostEstimate(flops=rows * width, bytes_accessed=6 * rows * width, transcendentals=0),
        name="lay",
    )(half, x, *earlier)


def sum_over_devices(keep, give, first_piece, second, send_second, others):
    f32, bf16 = jnp.float32, jnp.bfloat16
    region, slab = (lax.axis_index(axis).astype(jnp.uint32) for axis in ("region", "slab"))
    x = region & (SIDE - 1)
    z, core = slab >> 1, slab & 1
    width = keep.shape[1]

    def along_z(a, by):
        return lax.ppermute(a, "slab", [(p * 2 + c, (p + by) % SIDE * 2 + c) for p in range(SIDE) for c in range(2)])

    def along_x(a, by):
        return lax.ppermute(a, "region", [(p * SIDE + i, p * SIDE + (i + by) % SIDE) for p in range(SIDE) for i in range(SIDE)])

    def along_y(a, by):
        return lax.ppermute(a, "region", [(i * SIDE + p, (i + by) % SIDE * SIDE + p) for p in range(SIDE) for i in range(SIDE)])

    def swap(a):
        return lax.ppermute(a, "slab", [(p * 2 + c, p * 2 + 1 - c) for p in range(SIDE) for c in range(2)])

    def scatter(a, move, place):
        parts = a.reshape(SIDE, a.shape[0] // SIDE, width)
        got = [move(pick(parts, (place + by) & (SIDE - 1)).astype(bf16), by).astype(f32) for by in range(1, SIDE)]
        return pick(parts, place) + (got[0] + got[1] + got[2])

    def gather(a, move, place):
        got = [a] + [move(a, by) for by in range(1, SIDE)]
        stacked = jnp.stack(got)
        parts = [pick(stacked, (place - i) & (SIDE - 1)) for i in range(SIDE)]
        return jnp.concatenate(parts, axis=0)

    part = keep + swap(give).astype(f32)
    part = scatter(part, along_z, z)
    part = after(scatter(after(part, second), along_x, x).astype(bf16), first_piece)
    ring = [part.astype(f32)] + [along_y(part, by).astype(f32) for by in range(1, SIDE)]
    part = ((ring[0] + ring[2]) + (ring[1] + ring[3])).astype(bf16)
    part = gather(part, along_x, x)
    second_piece = send_second(part)
    part = gather(part, along_z, z)
    mine = core.astype(jnp.int32).reshape(1)
    laid = lay(mine, part)
    other = swap(after(part, second_piece, laid, *others))
    return lay(1 - mine, other, (laid,)), second_piece


def per_device(
    volume, patches, requests, lists, counts, w_query, key_weight, value_weight, w_out, cotangent
):
    f32 = jnp.float32
    bf16 = jnp.bfloat16
    width = volume.shape[1]
    head_dim = width // HEADS
    owned = patches.shape[0] // BLOCK
    asked = lax.all_to_all(requests.reshape(-1), "region", split_axis=0, concat_axis=0, tiled=True)
    outgoing = patches.reshape(owned, BLOCK, width)[asked]
    blocks = lax.all_to_all(outgoing, "region", split_axis=0, concat_axis=0, tiled=True)

    query = (nn(volume, w_query).astype(bf16) * head_dim ** -0.5).astype(bf16)
    grad_att = nt(cotangent, w_out).astype(bf16)

    core = (lax.axis_index("slab") & 1).reshape(1)
    w_both = jnp.concatenate([key_weight, value_weight], axis=1)
    attended, grad_query, keep, give, first, late = attention(
        lists, counts, core, query, grad_att, cotangent, blocks, key_weight, value_weight
    )
    returned = lax.all_to_all(first, "region", split_axis=0, concat_axis=0, tiled=True)

    second = nt(late.reshape(-1, late.shape[2]), w_both).astype(bf16).reshape(first.shape)
    mixed = nn(attended, w_out).astype(bf16)
    grad_volume = nt(grad_query, w_query).astype(bf16)
    patches_piece = settle(asked, returned, owned, 0)

    def send_second(summed):
        return lax.all_to_all(after(second, summed), "region", split_axis=0, concat_axis=0, tiled=True)

    grad_out_weight, later = sum_over_devices(
        keep, give, returned, second, send_second, (mixed, grad_volume, patches_piece)
    )
    grad_patches = settle(asked, later, owned, 1, (patches_piece,))
    return mixed, grad_volume, grad_patches.reshape(owned * BLOCK, width), grad_out_weight


def solution(mesh):
    rows = P(("region", "slab"), None)
    in_specs = (
        rows, rows, P(("region", "slab"), None, None), rows, P(("region", "slab")),
        P(), P(), P(), P(), rows,
    )
    return jax.shard_map(
        per_device, mesh=mesh, in_specs=in_specs, out_specs=(rows, rows, rows, P()), check_vma=False
    )
```

```python
import jax
import jax.numpy as jnp
from jax import lax
from jax.experimental import pallas as pl
from jax.experimental.pallas import tpu as pltpu
from jax.sharding import PartitionSpec as P

HEADS = 16
BLOCK = 128
QUAD = 4
BATCH = 2
RETURN_BATCH = 4
SIDE = 4
PIECES = 2
MIB = 2**20


def nt(a, b):
    return lax.dot_general(a, b, (((1,), (1,)), ((), ())), preferred_element_type=jnp.float32)


def nn(a, b):
    return lax.dot_general(a, b, (((1,), (0,)), ((), ())), preferred_element_type=jnp.float32)


def attention_kernel(
    lists_ref, counts_ref, core_ref, q_hbm, ga_hbm, cot_hbm, x_hbm, wk_hbm, wv_hbm,
    att_hbm, gq_hbm, keep_hbm, give_hbm, ret_hbm, late_hbm,
    att_ref, gq_ref, keep_ref, give_ref, late_ref, q_ref, ga_ref, cot_ref, att_t_ref, x_ref, wk_ref, wv_ref, k_ref, v_ref, kt_ref, vt_ref, acc_ref,
    mask_ref, used_ref, order_ref, in_sems, x_sems, out_sems, result_sems,
):
    bf16 = jnp.bfloat16
    slots, quads, rows, wide = k_ref.shape
    groups, listed = lists_ref.shape
    per_group = q_ref.shape[0] // groups
    head_dim = wide // QUAD

    loads = [
        pltpu.make_async_copy(src, dst, in_sems.at[i])
        for i, (src, dst) in enumerate(
            ((wk_hbm, wk_ref), (wv_hbm, wv_ref), (q_hbm, q_ref), (ga_hbm, ga_ref), (cot_hbm, cot_ref))
        )
    ]
    loads[0].start()

    for s in range(slots):
        used_ref[s] = 0
    for g in range(groups):
        for j in range(listed):
            s = lists_ref[g, j]
            used_ref[s] = used_ref[s] | (j < counts_ref[g]).astype(jnp.int32)
    n_used = jnp.int32(0)
    for s in range(slots):
        order_ref[n_used] = s
        n_used = n_used + used_ref[s]
    n = n_used
    for s in range(slots):
        order_ref[n] = s
        n = n + 1 - used_ref[s]
    batches = (n_used + BATCH - 1) // BATCH

    def bring(i):
        s = order_ref[i]
        return pltpu.make_async_copy(x_hbm.at[s], x_ref.at[s], x_sems.at[i])

    def ask(i, carry):
        bring(i).start()
        return carry

    lax.fori_loop(0, batches * BATCH, ask, 0)
    for load in loads[1:]:
        load.start()

    def clear(s, carry):
        acc_ref[s] = jnp.zeros(acc_ref.shape[1:], acc_ref.dtype)
        return carry

    lax.fori_loop(0, slots, clear, 0)

    def project(w_ref, out_ref, out_t_ref, first):
        def batch(b, carry):
            if first:
                for i in range(BATCH):
                    bring(b * BATCH + i).wait()
            ids = [order_ref[b * BATCH + i] for i in range(BATCH)]
            x = jnp.concatenate([x_ref[s] for s in ids], axis=0)
            for quad in range(quads):
                y = nn(x, w_ref[:, quad * wide:(quad + 1) * wide]).astype(bf16)
                for i, s in enumerate(ids):
                    part = y[i * rows:(i + 1) * rows]
                    out_ref[s, quad] = part
                    out_t_ref[s, quad] = part.T
            return carry

        lax.fori_loop(0, batches, batch, 0)

    loads[0].wait()
    project(wk_ref, k_ref, kt_ref, True)
    loads[1].wait()
    project(wv_ref, v_ref, vt_ref, False)
    for load in loads[2:]:
        load.wait()

    head_of_row = lax.broadcasted_iota(jnp.int32, mask_ref.shape, 0) // per_group
    head_of_lane = lax.broadcasted_iota(jnp.int32, mask_ref.shape, 1) // head_dim
    mask_ref[...] = (head_of_row == head_of_lane).astype(jnp.float32).astype(bf16)

    def spread(x):
        return jnp.concatenate([x] * QUAD, axis=0) * mask_ref[...]

    def diagonal(y):
        blocks = [
            y[h * head_dim:(h + 1) * head_dim, h * per_group:(h + 1) * per_group] for h in range(QUAD)
        ]
        return [jnp.concatenate(blocks[h:h + 2], axis=0) for h in range(0, QUAD, 2)]

    def step(i, carry):
        g = i // quads
        c = i % quads
        count = counts_ref[g]
        slot = [lists_ref[g, 0]] + [
            jnp.where(j < count, lists_ref[g, j], lists_ref[g, 0]) for j in range(1, listed)
        ]
        at_rows = pl.ds(pl.multiple_of(g * per_group, per_group), per_group)
        at_cols = pl.ds(pl.multiple_of(c * wide, wide), wide)
        k4 = jnp.concatenate([k_ref[s, c] for s in slot], axis=0)
        v4 = jnp.concatenate([v_ref[s, c] for s in slot], axis=0)
        kt4 = jnp.concatenate([kt_ref[s, c] for s in slot], axis=1)
        vt4 = jnp.concatenate([vt_ref[s, c] for s in slot], axis=1)
        q4 = spread(q_ref[at_rows, at_cols])
        g4 = spread(ga_ref[at_rows, at_cols])
        scores = nt(k4, q4)
        limits = [jnp.where(j < count, 3e38, -1e30) for j in range(listed)]
        scores = jnp.concatenate(
            [jnp.minimum(scores[j * rows:(j + 1) * rows], limits[j]) for j in range(listed)], axis=0
        )
        top = jnp.max(scores, axis=0, keepdims=True)
        expd = jnp.exp(scores - top)
        inverse = 1.0 / jnp.sum(expd, axis=0, keepdims=True)
        grad_prob = nt(v4, g4)
        delta = jnp.sum(expd * grad_prob, axis=0, keepdims=True) * inverse
        probs = expd * inverse
        grad_score = (probs * (grad_prob - delta)).astype(bf16)
        probs_b = probs.astype(bf16)
        def paired(wt, p):
            blocks = []
            for h in range(0, QUAD, 2):
                y = nn(wt[h * head_dim:(h + 2) * head_dim], p[:, h * per_group:(h + 2) * per_group])
                blocks.append(
                    jnp.concatenate([y[:head_dim, :per_group], y[head_dim:, per_group:]], axis=0)
                )
            return blocks

        att_parts = paired(vt4, probs_b)
        att_ref[at_rows, at_cols] = jnp.concatenate([y.T for y in att_parts], axis=1).astype(bf16)
        att_t_ref[at_cols, at_rows] = jnp.concatenate(att_parts, axis=0).astype(bf16)
        gq_parts = paired(kt4, grad_score)
        gq_ref[at_rows, at_cols] = (jnp.concatenate([y.T for y in gq_parts], axis=1) * head_dim ** -0.5).astype(bf16)
        grad_key = nn(grad_score, q4)
        grad_value = nn(probs_b, g4)
        for j in range(listed):
            s = slot[j]
            acc_ref[s, c] += grad_key[j * rows:(j + 1) * rows]
            acc_ref[s, quads + c] += grad_value[j * rows:(j + 1) * rows]
        return carry

    lax.fori_loop(0, groups * quads, step, 0, unroll=8)

    results = [
        pltpu.make_async_copy(src, dst, result_sems.at[i])
        for i, (src, dst) in enumerate(
            ((att_ref, att_hbm), (gq_ref, gq_hbm), (keep_ref, keep_hbm), (give_ref, give_hbm))
        )
    ]
    for result in results[:2]:
        result.start()

    half = keep_ref.shape[0]
    core = core_ref[0]
    for out_ref, mine in ((keep_ref, core), (give_ref, 1 - core)):
        for c in range(half // wide):
            at = pl.ds(pl.multiple_of(mine * half + c * wide, wide), wide)
            out_ref[c * wide:(c + 1) * wide, :] = nn(att_t_ref[at, :], cot_ref[...]).astype(out_ref.dtype)
    for result in results[2:]:
        result.start()

    cut = rows // PIECES

    def send(i, s):
        return [
            pltpu.make_async_copy(x_ref.at[s, pl.ds(0, cut)], ret_hbm.at[s], out_sems.at[i, 0]),
            pltpu.make_async_copy(late_ref.at[s], late_hbm.at[s], out_sems.at[i, 1]),
        ]

    def turn_back(b, carry):
        ids = [order_ref[b * RETURN_BATCH + i] for i in range(RETURN_BATCH)]
        grads = [
            jnp.concatenate(
                [
                    jnp.concatenate([acc_ref[s, at + c, :cut].astype(bf16) for c in range(quads)], axis=1)
                    for s in ids
                ],
                axis=0,
            )
            for at in (0, quads)
        ]
        for c in range(quads):
            out_rows = slice(c * wide, (c + 1) * wide)
            y = (nt(grads[0], wk_ref[out_rows]) + nt(grads[1], wv_ref[out_rows])).astype(bf16)
            for i, s in enumerate(ids):
                x_ref[s, :cut, out_rows] = y[i * cut:(i + 1) * cut]
        for i, s in enumerate(ids):
            for c in range(2 * quads):
                late_ref[s, :, c * wide:(c + 1) * wide] = acc_ref[s, c, cut:].astype(bf16)
            for copy in send(b * RETURN_BATCH + i, s):
                copy.start()
        return carry

    batches = (n_used + RETURN_BATCH - 1) // RETURN_BATCH
    lax.fori_loop(0, batches, turn_back, 0)

    def nothing(i, carry):
        s = order_ref[i]
        x_ref[s, :cut] = jnp.zeros((cut,) + x_ref.shape[2:], x_ref.dtype)
        late_ref[s] = jnp.zeros(late_ref.shape[1:], late_ref.dtype)
        for copy in send(i, s):
            copy.start()
        return carry

    lax.fori_loop(batches * RETURN_BATCH, slots, nothing, 0)

    def arrive(i, carry):
        for copy in send(i, order_ref[i]):
            copy.wait()
        return carry

    lax.fori_loop(0, slots, arrive, 0)
    for result in results:
        result.wait()


def attention(lists, counts, core, q, ga, cot, x, wk, wv):
    bf16 = jnp.bfloat16
    slots, rows, width = x.shape
    quads = HEADS // QUAD
    wide = width // quads
    smem = pl.BlockSpec(memory_space=pltpu.SMEM)
    hbm = pl.BlockSpec(memory_space=pl.ANY)
    scores = HEADS * q.shape[0] * lists.shape[1] * rows
    straight = pltpu.VMEM((slots, quads, rows, wide), bf16)
    turned = pltpu.VMEM((slots, quads, wide, rows), bf16)
    return pl.pallas_call(
        attention_kernel,
        in_specs=[smem] * 3 + [hbm] * 6,
        out_specs=[hbm] * 6,
        out_shape=[
            jax.ShapeDtypeStruct(q.shape, bf16),
            jax.ShapeDtypeStruct(q.shape, bf16),
            jax.ShapeDtypeStruct((width // 2, width), jnp.float32),
            jax.ShapeDtypeStruct((width // 2, width), bf16),
            jax.ShapeDtypeStruct((slots, rows // PIECES, width), bf16),
            jax.ShapeDtypeStruct((slots, rows // PIECES, 2 * width), bf16),
        ],
        scratch_shapes=[
            pltpu.VMEM(q.shape, bf16), pltpu.VMEM(q.shape, bf16),
            pltpu.VMEM((width // 2, width), jnp.float32), pltpu.VMEM((width // 2, width), bf16),
            pltpu.VMEM((slots, rows // PIECES, 2 * width), bf16),
            pltpu.VMEM(q.shape, bf16), pltpu.VMEM(q.shape, bf16), pltpu.VMEM(q.shape, bf16),
            pltpu.VMEM(q.shape[::-1], bf16), pltpu.VMEM(x.shape, bf16),
            pltpu.VMEM(wk.shape, bf16), pltpu.VMEM(wv.shape, bf16),
            straight, straight, turned, turned,
            pltpu.VMEM((slots, 2 * quads, rows, wide), jnp.float32),
            pltpu.VMEM((QUAD * (q.shape[0] // lists.shape[0]), wide), bf16),
            pltpu.SMEM((slots + 1,), jnp.int32),
            pltpu.SMEM((slots + 1,), jnp.int32),
            pltpu.SemaphoreType.DMA((5,)),
            pltpu.SemaphoreType.DMA((slots,)),
            pltpu.SemaphoreType.DMA((slots, PIECES)),
            pltpu.SemaphoreType.DMA((4,)),
        ],
        compiler_params=pltpu.CompilerParams(vmem_limit_bytes=62 * MIB),
        cost_estimate=pl.CostEstimate(
            flops=12 * scores * wide + 8 * slots * rows * width * width,
            bytes_accessed=20 * MIB, transcendentals=scores,
        ),
        name="attention",
    )(lists, counts, core, q, ga, cot, x, wk, wv)


def settle_kernel(asked_ref, x_ref, *refs):
    out_ref, acc_ref = refs[-2:]
    acc_ref[...] = jnp.zeros_like(acc_ref)
    for p in range(x_ref.shape[0]):
        acc_ref[asked_ref[p]] += x_ref[p].astype(jnp.float32)
    out_ref[...] = acc_ref[...].astype(out_ref.dtype)


def settle(asked, x, owned, piece, earlier=()):
    slots, rows, width = x.shape
    cut = 16
    first = piece * (rows // cut)
    return pl.pallas_call(
        settle_kernel,
        grid=(rows // cut,),
        in_specs=[
            pl.BlockSpec(memory_space=pltpu.SMEM),
            pl.BlockSpec((slots, cut, width), lambda i: (0, i, 0)),
        ] + [pl.BlockSpec(memory_space=pl.ANY)] * len(earlier),
        out_specs=pl.BlockSpec((owned, cut, width), lambda i: (0, first + i, 0)),
        out_shape=jax.ShapeDtypeStruct((owned, rows * PIECES, width), jnp.bfloat16),
        scratch_shapes=[pltpu.VMEM((owned, cut, width), jnp.float32)],
        input_output_aliases={2: 0} if earlier else {},
        compiler_params=pltpu.CompilerParams(vmem_limit_bytes=16 * MIB),
        cost_estimate=pl.CostEstimate(flops=slots * rows * width, bytes_accessed=3 * slots * rows * width, transcendentals=0),
        name="settle",
    )(asked, x, *earlier)


def pick(parts, index):
    start = [index.astype(jnp.uint32)] + [jnp.uint32(0)] * (parts.ndim - 1)
    return lax.dynamic_slice(parts, start, (1,) + parts.shape[1:])[0]


def after(a, *others):
    return lax.optimization_barrier((a,) + others)[0]


def lay_kernel(half_ref, x_ref, *refs):
    refs[-1][...] = x_ref[...].astype(refs[-1].dtype)


def lay(half, x, total, at=0, earlier=()):
    rows, width = x.shape
    cut = 128
    per_half, first = total // 2 // cut, at // cut
    return pl.pallas_call(
        lay_kernel,
        grid_spec=pltpu.PrefetchScalarGridSpec(
            num_scalar_prefetch=1,
            grid=(rows // cut,),
            in_specs=[pl.BlockSpec((cut, width), lambda i, half_ref: (i, 0))]
            + [pl.BlockSpec(memory_space=pl.ANY)] * len(earlier),
            out_specs=pl.BlockSpec((cut, width), lambda i, half_ref: (half_ref[0] * per_half + first + i, 0)),
        ),
        out_shape=jax.ShapeDtypeStruct((total, width), jnp.float32),
        input_output_aliases={2: 0} if earlier else {},
        compiler_params=pltpu.CompilerParams(vmem_limit_bytes=16 * MIB),
        cost_estimate=pl.CostEstimate(flops=rows * width, bytes_accessed=6 * rows * width, transcendentals=0),
        name="lay",
    )(half, x, *earlier)


def sum_over_devices(keep, give, first_piece, second, send_second, others):
    f32, bf16 = jnp.float32, jnp.bfloat16
    region, slab = (lax.axis_index(axis).astype(jnp.uint32) for axis in ("region", "slab"))
    x = region & (SIDE - 1)
    z, core = slab >> 1, slab & 1
    width = keep.shape[1]

    def along_z(a, by):
        return lax.ppermute(a, "slab", [(p * 2 + c, (p + by) % SIDE * 2 + c) for p in range(SIDE) for c in range(2)])

    def along_x(a, by):
        return lax.ppermute(a, "region", [(p * SIDE + i, p * SIDE + (i + by) % SIDE) for p in range(SIDE) for i in range(SIDE)])

    def along_y(a, by):
        return lax.ppermute(a, "region", [(i * SIDE + p, (i + by) % SIDE * SIDE + p) for p in range(SIDE) for i in range(SIDE)])

    def swap(a):
        return lax.ppermute(a, "slab", [(p * 2 + c, p * 2 + 1 - c) for p in range(SIDE) for c in range(2)])

    def scatter(a, move, place):
        parts = a.reshape(SIDE, a.shape[0] // SIDE, width)
        got = [move(pick(parts, (place + by) & (SIDE - 1)).astype(bf16), by).astype(f32) for by in range(1, SIDE)]
        return pick(parts, place) + (got[0] + got[1] + got[2])

    def gather(a, move, place):
        got = [a] + [move(a, by) for by in range(1, SIDE)]
        stacked = jnp.stack(got)
        parts = [pick(stacked, (place - i) & (SIDE - 1)) for i in range(SIDE)]
        return jnp.concatenate(parts, axis=0)

    part = keep + swap(give).astype(f32)
    part = scatter(part, along_z, z)
    part = after(scatter(after(part, second), along_x, x).astype(bf16), first_piece)
    ring = [part.astype(f32)] + [along_y(part, by).astype(f32) for by in range(1, SIDE)]
    part = ((ring[0] + ring[2]) + (ring[1] + ring[3])).astype(bf16)
    part = gather(part, along_x, x)
    second_piece = send_second(part)
    part = gather(part, along_z, z)
    mine = core.astype(jnp.int32).reshape(1)
    total, most = 2 * part.shape[0], part.shape[0] * 3 // 4
    laid = lay(mine, part, total)
    laid = lay(1 - mine, swap(part[:most]), total, 0, (laid,))
    other = swap(after(part[most:], second_piece, laid, *others))
    return lay(1 - mine, other, total, most, (laid,)), second_piece


def per_device(
    volume, patches, requests, lists, counts, w_query, key_weight, value_weight, w_out, cotangent
):
    f32 = jnp.float32
    bf16 = jnp.bfloat16
    width = volume.shape[1]
    head_dim = width // HEADS
    owned = patches.shape[0] // BLOCK
    asked = lax.all_to_all(requests.reshape(-1), "region", split_axis=0, concat_axis=0, tiled=True)
    outgoing = patches.reshape(owned, BLOCK, width)[asked]
    blocks = lax.all_to_all(outgoing, "region", split_axis=0, concat_axis=0, tiled=True)

    query = (nn(volume, w_query).astype(bf16) * head_dim ** -0.5).astype(bf16)
    grad_att = nt(cotangent, w_out).astype(bf16)

    core = (lax.axis_index("slab") & 1).reshape(1)
    w_both = jnp.concatenate([key_weight, value_weight], axis=1)
    attended, grad_query, keep, give, first, late = attention(
        lists, counts, core, query, grad_att, cotangent, blocks, key_weight, value_weight
    )
    returned = lax.all_to_all(first, "region", split_axis=0, concat_axis=0, tiled=True)

    second = nt(late.reshape(-1, late.shape[2]), w_both).astype(bf16).reshape(first.shape)
    mixed = nn(attended, w_out).astype(bf16)
    grad_volume = nt(grad_query, w_query).astype(bf16)
    patches_piece = settle(asked, returned, owned, 0)

    def send_second(summed):
        return lax.all_to_all(after(second, summed), "region", split_axis=0, concat_axis=0, tiled=True)

    grad_out_weight, later = sum_over_devices(
        keep, give, returned, second, send_second, (mixed, grad_volume, patches_piece)
    )
    grad_patches = settle(asked, later, owned, 1, (patches_piece,))
    return mixed, grad_volume, grad_patches.reshape(owned * BLOCK, width), grad_out_weight


def solution(mesh):
    rows = P(("region", "slab"), None)
    in_specs = (
        rows, rows, P(("region", "slab"), None, None), rows, P(("region", "slab")),
        P(), P(), P(), P(), rows,
    )
    return jax.shard_map(
        per_device, mesh=mesh, in_specs=in_specs, out_specs=(rows, rows, rows, P()), check_vma=False
    )
```
